32 devices in a mesh: dp: 8 (over z, y), head: 4 (over x, core).
Axes of the slice: x: 2, y: 2, z: 4, core: 2. Of those that a mesh axis runs over, the one named last changes fastest.
Arguments:
- tokens: bfloat16 [16384, 2048], P(('dp', 'head')), may hold values from -6 to 6
- norm_gain: bfloat16 [2048], replicated, may hold values from 0.5 to 1.5
- w_proj: bfloat16 [4, 2048, 2048], P(None, None, 'head'), may hold values from -0.125 to 0.125
- w_beta: bfloat16 [2048, 16], P(None, 'head'), may hold values from -0.125 to 0.125
- conv_weight: bfloat16 [3, 4, 2048], P(None, None, 'head'), may hold values from -3 to 3
- head_gain: bfloat16 [128], replicated, may hold values from 0.5 to 1.5
- w_out: bfloat16 [2048, 2048], P('head'), may hold values from -0.125 to 0.125
- ffn_gain: bfloat16 [2048], replicated, may hold values from 0.5 to 1.5
- w_ffn: bfloat16 [2, 2048, 5632], P(None, None, 'head'), may hold values from -0.125 to 0.125
- w_down: bfloat16 [5632, 2048], P('head'), may hold values from -0.078125 to 0.078125
- group_ids: int32 [16], P('dp'), may hold values from 0 to 3, as said below
- group_weight: int32 [4], replicated, may hold values from 1 to 3
- cotangent: bfloat16 [16384, 2048], P(('dp', 'head')), may hold values from -6 to 6
Outputs:
- mixed_out: bfloat16 [16384, 2048], P(('dp', 'head'))
- grad_tokens: float32 [16384, 2048], P(('dp', 'head'))
- grad_norm_gain: float32 [2048], replicated
- grad_w_proj: float32 [4, 2048, 2048], P(None, 'dp', 'head')
- grad_w_beta: float32 [2048, 16], P(None, 'head')
- grad_conv_weight: float32 [3, 4, 2048], P(None, None, 'head')
- grad_head_gain: float32 [128], replicated
- grad_w_out: float32 [2048, 2048], P('head', 'dp')
- grad_ffn_gain: float32 [2048], replicated
- grad_w_ffn: float32 [2, 2048, 5632], P(None, 'dp', 'head')
- grad_w_down: float32 [5632, 2048], P('head', 'dp')
The draws below stay inside these ranges and needn't reach their ends.
Inputs may be any that keep to these rules, and one draw needn't show every extreme that they name: `group_ids`: the domain group of a sequence; every group holds 2 sequences or more. `group_weight`: a positive integer weight of a group.
All inputs are finite; a program needn't handle non-finite values.
Results may differ from the reference program's by a relative error of at most 0.012.
The reference program's roundings to bfloat16 on the way count: a program that leaves them out, or rounds other values in their place, can miss the bound.
Values may be sent and summed in bfloat16 or wider, within the bound.
No kernel may reach another device: no remote copies, remote signals or barrier semaphores. Data moves between devices by JAX's collectives and lax.ppermute only.
A program may use at most 384 MiB of HBM per device.

```python
import jax
import jax.numpy as jnp
from jax import lax

D = 2048
HEADS = 16
HEAD_DIM = 128
FF = 5632
CONV = 4
SPAN = 64
LEN = 1024
GROUPS = 4
HK = 2048
SEQS = 16
TOKENS = 16384


def draw_group_ids(key, part):
    key = jax.random.fold_in(key, 11)
    order_key, rest_key = jax.random.split(key)
    order = jax.random.permutation(order_key, SEQS).astype(jnp.int32)
    free_pick = jax.random.randint(rest_key, (SEQS,), 0, GROUPS, dtype=jnp.int32)
    dealt = order % GROUPS
    return jnp.where(order < SEQS // 2, dealt, free_pick).astype(jnp.int32)


def set_ends(array, stream_key, least, largest):
    place = [jax.random.randint(jax.random.fold_in(stream_key, axis), (), 0, length) for axis, length in enumerate(array.shape)]
    main_axis = array.shape.index(max(array.shape))
    beside = place[:main_axis] + [(place[main_axis] + 1) % array.shape[main_axis]] + place[main_axis + 1:]
    return array.at[tuple(place)].set(least).at[tuple(beside)].set(largest)


def raised(values, key, source, target, shards_of, factor):
    owner, partner = [(jnp.arange(values.shape[dim]) // (values.shape[dim] // shards_of)).reshape([-1 if axis == dim else 1 for axis in range(values.ndim)]) for dim in (source, target)]
    chosen = jax.random.permutation(key, shards_of)[partner]
    strong = (owner == chosen) | (owner == (partner + shards_of // 2) % shards_of)
    return jnp.where(strong, factor * values, values)


def block_scale(own_key, dims, pieces, low, high):
    level, own = 1.0, jax.random.fold_in(own_key, 6)
    for dim, parts in pieces:
        draws = jnp.exp(jax.random.uniform(jax.random.fold_in(own, dim), (parts,), jnp.float32, low / len(pieces), high / len(pieces)))
        level = level * jnp.repeat(draws, dims[dim] // parts).reshape([-1 if axis == dim else 1 for axis in range(len(dims))])
    return level


def normal_values(own_key, extent, scale, bound, cuts=(), kind=jnp.bfloat16):
    array = scale * jax.random.normal(own_key, extent, jnp.float32)
    if cuts:
        array = array * block_scale(own_key, extent, cuts, -0.22, 0.18)
    return jnp.clip(array, -bound, bound).astype(kind)


def noise_with(stream_key, extent, deviation, reach, cuts, heavy, held_as=jnp.bfloat16):
    values = deviation * jax.random.normal(stream_key, extent, jnp.float32)
    if cuts:
        values = values * block_scale(stream_key, extent, cuts, -0.22, 0.18)
    return jnp.clip(raised(values, jax.random.fold_in(stream_key, 3), *heavy), -reach, reach).astype(held_as)


def setup_inputs(seed: int = 0) -> dict:
    streams_of = jax.random.split(jax.random.key(seed), 14)
    return {
        "tokens": normal_values(streams_of[0], (TOKENS, D), 1.0, 6.0, ((0, 32),)),
        "norm_gain": jnp.clip(1.0 + 0.1 * jax.random.normal(streams_of[1], (D,), jnp.float32), 0.5, 1.5).astype(jnp.bfloat16),
        "w_proj": normal_values(streams_of[2], (4, D, HK), D ** -0.5, 0.125, ((2, 4),)),
        "w_beta": normal_values(streams_of[3], (D, HEADS), D ** -0.5, 0.125, ((1, 4),)),
        "conv_weight": normal_values(streams_of[4], (3, CONV, HK), CONV ** -0.5, 3.0, ((2, 4),)),
        "head_gain": jnp.clip(1.0 + 0.1 * jax.random.normal(streams_of[5], (HEAD_DIM,), jnp.float32), 0.5, 1.5).astype(jnp.bfloat16),
        "w_out": normal_values(streams_of[6], (HK, D), HK ** -0.5, 0.125, ((0, 4),)),
        "ffn_gain": jnp.clip(1.0 + 0.1 * jax.random.normal(streams_of[7], (D,), jnp.float32), 0.5, 1.5).astype(jnp.bfloat16),
        "w_ffn": normal_values(streams_of[8], (2, D, FF), D ** -0.5, 0.125, ((2, 4),)),
        "w_down": normal_values(streams_of[9], (FF, D), FF ** -0.5, 0.078125, ((0, 4),)),
        "group_ids": draw_group_ids(jax.random.fold_in(streams_of[13], 71), 0),
        "group_weight": set_ends(jax.random.randint(streams_of[11], (GROUPS,), 1, 4), jax.random.fold_in(streams_of[11], 1), 1, 3).astype(jnp.int32),
        "cotangent": noise_with(streams_of[12], (TOKENS, D), 1.0, 6.0, ((0, 32),), (0, 1, 32, 2.75)),
    }


EPS = 1e-06

@jax.custom_vjp
def low(v):
    return lax.optimization_barrier(v.astype(jnp.bfloat16)).astype(jnp.float32)

@jax.custom_vjp
def low_back(v):
    return v

def low_keep(v):
    return (low(v), None)

def low_pass(kept, grad):
    return (grad,)

def back_keep(v):
    return (v, None)

def back_low(kept, grad):
    return (low(grad),)
low.defvjp(low_keep, low_pass)
low_back.defvjp(back_keep, back_low)

def rms_scale(signal, gain):
    return signal * lax.rsqrt(lax.optimization_barrier(jnp.mean(signal * signal, axis=-1, keepdims=True)) + EPS) * gain

def causal_conv(signal, kernel):
    kernel_taps = kernel.shape[0]
    pad_widths = [(0, 0)] * (signal.ndim - 2) + [(kernel_taps - 1, 0), (0, 0)]
    padded = jnp.pad(signal, pad_widths)
    length = signal.shape[-2]
    summed = jnp.zeros_like(signal)
    for offset in range(kernel_taps):
        summed = summed + kernel[offset] * lax.slice_in_dim(padded, offset, offset + length, axis=signal.ndim - 2)
    return summed

def span_step(carried_state, block):
    query_rows, key_matrix, values, beta_rows = block
    largest_entry = lax.Precision.HIGHEST
    head_width = key_matrix.shape[-1]
    block_len = key_matrix.shape[-2]
    keyed = key_matrix * beta_rows[..., None]
    gram_rows = jnp.einsum('hik,hjk->hij', keyed, key_matrix, precision=largest_entry)
    unit_lower = jnp.tril(gram_rows, -1) + jnp.eye(block_len, dtype=gram_rows.dtype)
    stacked = jnp.concatenate([keyed, values * beta_rows[..., None]], axis=-1)
    triangular_solution = jax.scipy.linalg.solve_triangular(unit_lower, stacked, lower=True, unit_diagonal=True)
    adjusted_values = triangular_solution[..., head_width:] - jnp.einsum('ruz,rzm->rum', triangular_solution[..., :head_width], carried_state, precision=largest_entry)
    attention_scores = jnp.tril(jnp.einsum('hik,hjk->hij', query_rows, key_matrix, precision=largest_entry))
    output_rows = jnp.einsum('ruz,rzm->rum', query_rows, carried_state, precision=largest_entry) + jnp.einsum('lxb,lbc->lxc', attention_scores, adjusted_values, precision=largest_entry)
    carried_state = carried_state + jnp.einsum('ugo,ugd->uod', key_matrix, adjusted_values, precision=largest_entry)
    return (carried_state, output_rows)

def delta_rule(query_rows, key_matrix, values, beta_rows):
    batch_rows, length, head_width = query_rows.shape
    blocks = length // SPAN

    def to_blocks(tensor):
        shaped = tensor.reshape((batch_rows, blocks, SPAN) + tensor.shape[2:])
        return jnp.moveaxis(shaped, 1, 0)
    initial = jnp.zeros((batch_rows, head_width, head_width), jnp.float32)
    _, outputs = lax.scan(jax.checkpoint(span_step), initial, (to_blocks(query_rows), to_blocks(key_matrix), to_blocks(values), to_blocks(beta_rows)))
    return jnp.moveaxis(outputs, 0, 1).reshape(batch_rows, length, head_width)

def to_heads(tensor):
    seq_count, length, channels = tensor.shape
    shaped = tensor.reshape(seq_count, length, channels // HEAD_DIM, HEAD_DIM)
    return shaped.transpose(0, 2, 1, 3).reshape(-1, length, HEAD_DIM)

def prepare(projected, beta_logit, conv_float):
    activated = [jax.nn.silu(causal_conv(projected[position], conv_float[position])) for position in range(3)]
    seq_count, length, channels = activated[1].shape
    key_heads = activated[1].reshape(seq_count, length, channels // HEAD_DIM, HEAD_DIM)
    key_unit = key_heads * lax.rsqrt(lax.optimization_barrier(jnp.sum(key_heads * key_heads, axis=-1, keepdims=True)) + EPS)
    return (activated[0], key_unit.reshape(seq_count, length, channels), activated[2], jax.nn.sigmoid(beta_logit))

def mix(query_rows, key_matrix, values, beta, gate_rows, gain_heads):
    seq_count, length, channels = query_rows.shape
    beta_rows = beta.transpose(0, 2, 1).reshape(-1, length)
    outputs = delta_rule(to_heads(query_rows), to_heads(key_matrix), to_heads(values), beta_rows)
    outputs = outputs.reshape(seq_count, channels // HEAD_DIM, length, HEAD_DIM).transpose(0, 2, 1, 3)
    gates = gate_rows.reshape(seq_count, length, channels // HEAD_DIM, HEAD_DIM)
    normed = outputs * lax.rsqrt(lax.optimization_barrier(jnp.mean(outputs * outputs, axis=-1, keepdims=True)) + EPS) * gain_heads * jax.nn.silu(gates)
    return normed.reshape(seq_count, length, channels)

def layer(x_rows, norm_gain, w_proj, w_beta, conv_weight, head_gain, w_out, ffn_gain, w_ffn, w_down):
    largest_entry = lax.Precision.HIGHEST
    normed = low(rms_scale(x_rows, norm_gain))
    projected = low_back(jnp.einsum('td,fdk->ftk', normed, w_proj, precision=largest_entry))
    beta_logit = low_back(jnp.dot(normed, w_beta, precision=largest_entry))
    seq_proj = projected[:, None]
    query_rows, key_matrix, values, beta = prepare(seq_proj[:3], beta_logit[None], conv_weight)
    gated = mix(low(query_rows), low(key_matrix), low(values), beta, seq_proj[3], head_gain)
    flat_out = low(gated[0])
    mixer_out = low_back(jnp.dot(flat_out, w_out, precision=largest_entry))
    middle = x_rows + mixer_out
    normed_two = low(rms_scale(middle, ffn_gain))
    gate_up = low_back(jnp.einsum('td,fdk->ftk', normed_two, w_ffn, precision=largest_entry))
    hidden = low(jax.nn.silu(gate_up[0]) * gate_up[1])
    ffn_out = low_back(jnp.dot(hidden, w_down, precision=largest_entry))
    return middle + ffn_out

def reference(tokens, norm_gain, w_proj, w_beta, conv_weight, head_gain, w_out, ffn_gain, w_ffn, w_down, group_ids, group_weight, cotangent):
    weights = tuple((tensor.astype(jnp.float32) for tensor in (norm_gain, w_proj, w_beta, conv_weight, head_gain, w_out, ffn_gain, w_ffn, w_down)))
    group_range = jnp.arange(GROUPS, dtype=jnp.int32)
    member = (group_ids[:, None] == group_range[None, :]).astype(jnp.int32)
    counts = (lax.optimization_barrier(jnp.sum(member, axis=0)) * LEN).astype(jnp.float32)
    member_float = member.astype(jnp.float32)
    seq_weight = lax.optimization_barrier(jnp.sum(member_float * group_weight.astype(jnp.float32)[None, :], axis=1))
    seq_count = lax.optimization_barrier(jnp.sum(member_float * counts[None, :], axis=1))
    seq_scale = seq_weight * TOKENS / (GROUPS * seq_count)
    seq_total = group_ids.shape[0]
    x_seq = tokens.astype(jnp.float32).reshape(seq_total, LEN, -1)
    cot_seq = cotangent.astype(jnp.float32).reshape(seq_total, LEN, -1)

    def one_sequence(running, inputs):
        x_rows, cot_rows, factor = inputs
        result, pullback = jax.vjp(layer, x_rows, *weights)
        grads = pullback(cot_rows * factor)
        running = tuple((summed_grad + fresh_grad for summed_grad, fresh_grad in zip(running, grads[1:])))
        return (running, (result.astype(jnp.bfloat16), grads[0]))
    initial = tuple((jnp.zeros_like(tensor) for tensor in weights))
    summed, (results, grad_rows) = lax.scan(one_sequence, initial, (x_seq, cot_seq, seq_scale))
    return (results.reshape(TOKENS, -1), grad_rows.reshape(TOKENS, -1), summed[0], summed[1], summed[2], summed[3], summed[4], summed[5], summed[6], summed[7], summed[8])
```

```python
import functools

import jax
import jax.numpy as jnp
from jax import lax
from jax.experimental import pallas as pl
from jax.experimental.pallas import tpu as pltpu
from jax.sharding import PartitionSpec as P

HEAD_DIM = 128
CHUNK = 128
LEN = 1024
BACK_CHAINS = 4
GROUPS = 4
EPS = 1e-06
F32 = jnp.float32
BF16 = jnp.bfloat16
BRIEF = pl.CostEstimate(flops=10**9, bytes_accessed=10**6, transcendentals=0)


def narrow(value):
    return value.astype(BF16)


def dot_nn(left, right):
    return lax.dot_general(
        narrow(left), narrow(right), (((1,), (0,)), ((), ())), preferred_element_type=F32
    )


def dot_nt(left, right):
    return lax.dot_general(
        narrow(left), narrow(right), (((1,), (1,)), ((), ())), preferred_element_type=F32
    )


def dot_tn(left, right):
    return lax.dot_general(
        narrow(left), narrow(right), (((0,), (0,)), ((), ())), preferred_element_type=F32
    )


def sigmoid(value):
    return 1.0 / (1.0 + jnp.exp(-value))


def invert_lower(matrices, row, col):
    joined = row ^ col
    extras = [-jnp.where(joined == 1, below, 0.0) for below in matrices]
    size = 2
    while size < CHUNK:
        inside = (joined >= size) & (joined < 2 * size)
        corners = [jnp.where(inside, below, 0.0) for below in matrices]
        lefts = [corner + dot_nn(extra, corner) for extra, corner in zip(extras, corners)]
        extras = [extra - left - dot_nn(left, extra) for extra, left in zip(extras, lefts)]
        size *= 2
    rounded = [narrow(extra) for extra in extras]
    highs = [narrow(below) for below in matrices]
    lows = [narrow(below - high.astype(F32)) for below, high in zip(matrices, highs)]
    products = [
        dot_nn(jnp.concatenate([high, low], axis=1), jnp.concatenate([kept, kept], axis=0))
        for high, low, kept in zip(highs, lows, rounded)
    ]
    wides = [kept.astype(F32) for kept in rounded]
    residuals = [
        -(below + wide + product) for below, wide, product in zip(matrices, wides, products)
    ]
    return [
        wide + residual + dot_nn(kept, residual)
        for wide, residual, kept in zip(wides, residuals, rounded)
    ]


def activate_taps(padded, taps, position, seq, lanes):
    summed = None
    for offset in range(4):
        term = taps[position, offset : offset + 1, lanes] * padded[seq, position, pl.ds(5 + offset, CHUNK), lanes]
        summed = term if summed is None else summed + term
    return summed


def chains_of(seqs, heads):
    return [(seq, head, pl.ds(head * HEAD_DIM, HEAD_DIM)) for seq in range(seqs) for head in range(heads)]


def masks():
    row = lax.broadcasted_iota(jnp.int32, (CHUNK, CHUNK), 0)
    col = lax.broadcasted_iota(jnp.int32, (CHUNK, CHUNK), 1)
    return row, col


def forward_kernel(
    order,
    projected,
    logits,
    taps,
    gain,
    state_in,
    halo_in,
    gated,
    raw,
    inverse,
    states,
    adjusted,
    state_out,
    state,
    padded,
):
    step = pl.program_id(0)
    seqs, heads = state.shape[:2]
    chains = chains_of(seqs, heads)

    @pl.when(step == 0)
    def _():
        state[...] = state_in[...]
        padded[:, :, pl.ds(0, 8), :] = halo_in[...]

    @pl.when(step > 0)
    def _():
        padded[:, :, pl.ds(0, 8), :] = padded[:, :, pl.ds(CHUNK, 8), :]

    for seq in range(seqs):
        for position in range(3):
            padded[seq, position, pl.ds(8, CHUNK), :] = projected[position, 0, seq].astype(F32)
    row, col = masks()
    queries, keys, values, betas = [], [], [], []
    for seq, head, lanes in chains:
        acts = []
        for position in range(3):
            summed = activate_taps(padded, taps, position, seq, lanes)
            acts.append(summed * sigmoid(summed))
        scale = lax.rsqrt(jnp.sum(acts[1] * acts[1], axis=-1, keepdims=True) + EPS)
        queries.append(narrow(acts[0]))
        keys.append(narrow(acts[1] * scale))
        values.append(narrow(acts[2]))
        betas.append(sigmoid(logits[0, seq, :, head : head + 1]))
    belows = [jnp.where(row > col, beta * dot_nt(key, key), 0.0) for key, beta in zip(keys, betas)]
    scores = [
        narrow(jnp.where(row >= col, dot_nt(query, key), 0.0)) for query, key in zip(queries, keys)
    ]
    extras = [narrow(extra) for extra in invert_lower(belows, row, col)]
    nows = [state[seq, head] for seq, head, _ in chains]
    reads = []
    for query, key, now in zip(queries, keys, nows):
        high = narrow(now)
        low = narrow(now - high.astype(F32))
        read = dot_nn(jnp.concatenate([key, query], axis=0), jnp.concatenate([high, low], axis=1))
        reads.append(read[:, :HEAD_DIM] + read[:, HEAD_DIM:])
    targets = [
        beta * (value.astype(F32) - read[:CHUNK]) for beta, value, read in zip(betas, values, reads)
    ]
    updates = [narrow(target + dot_nn(extra, target)) for extra, target in zip(extras, targets)]
    outs = [
        read[CHUNK:] + dot_nn(score, update) for read, score, update in zip(reads, scores, updates)
    ]
    laters = [now + dot_tn(key, update) for now, key, update in zip(nows, keys, updates)]
    for index, (seq, head, lanes) in enumerate(chains):
        state[seq, head] = laters[index]
        raw[0, seq, :, lanes] = outs[index]
        inverse[0, seq, :, lanes] = extras[index].T
        states[0, seq, :, lanes] = nows[index]
        adjusted[0, seq, :, lanes] = updates[index]
        gate = projected[3, 0, seq, :, lanes].astype(F32)
        rate = lax.rsqrt(jnp.mean(outs[index] * outs[index], axis=-1, keepdims=True) + EPS)
        gated[0, seq, :, lanes] = narrow(outs[index] * rate * gain[...] * (gate * sigmoid(gate)))

    @pl.when(step == pl.num_programs(0) - 1)
    def _():
        state_out[...] = state[...]


def slope(value, sig):
    return sig * (1.0 + value * (1.0 - sig))


def fold_rows(value):
    return jnp.sum(value.reshape(CHUNK // 8, 8, value.shape[-1]), axis=0)


def backward_kernel(
    order,
    projected,
    before,
    logits,
    taps,
    gain,
    halo_in,
    grad_gated,
    raw,
    inverse,
    states,
    adjusted,
    grad_state_in,
    after_in,
    grad_projected,
    grad_logits,
    grad_taps,
    grad_gain,
    grad_state_out,
    after_out,
    grad_state,
    padded,
    trailing,
    taps_sum,
    gain_sum,
):
    step = pl.program_id(0)
    last = pl.num_programs(0) - 1
    seqs, heads = grad_state.shape[:2]

    @pl.when(step == 0)
    def _():
        taps_sum[...] = jnp.zeros_like(taps_sum)
        gain_sum[...] = jnp.zeros_like(gain_sum)
        grad_state[...] = grad_state_in[...]
        trailing[:, :, pl.ds(CHUNK, 8), :] = after_in[...]

    @pl.when(step > 0)
    def _():
        trailing[:, :, pl.ds(CHUNK, 8), :] = trailing[:, :, pl.ds(0, 8), :]

    @pl.when(step == last)
    def _():
        padded[:, :, pl.ds(0, 8), :] = halo_in[...]

    @pl.when(step < last)
    def _():
        for seq in range(seqs):
            for position in range(3):
                padded[seq, position, pl.ds(0, 8), :] = before[position, 0, seq].astype(F32)

    for seq in range(seqs):
        for position in range(3):
            padded[seq, position, pl.ds(8, CHUNK), :] = projected[position, 0, seq].astype(F32)
    row, col = masks()
    everything = chains_of(seqs, heads)
    for begin in range(0, len(everything), BACK_CHAINS):
        chains = everything[begin : begin + BACK_CHAINS]
        slopes, lengths, scales, queries, keys, values, betas = [], [], [], [], [], [], []
        for seq, head, lanes in chains:
            sums = [activate_taps(padded, taps, position, seq, lanes) for position in range(3)]
            sigs = [sigmoid(summed) for summed in sums]
            acts = [summed * sig for summed, sig in zip(sums, sigs)]
            slopes.append([slope(summed, sig) for summed, sig in zip(sums, sigs)])
            scale = lax.rsqrt(jnp.sum(acts[1] * acts[1], axis=-1, keepdims=True) + EPS)
            lengths.append(acts[1])
            scales.append(scale)
            queries.append(narrow(acts[0]))
            keys.append(narrow(acts[1] * scale))
            values.append(narrow(acts[2]))
            betas.append(sigmoid(logits[0, seq, :, head : head + 1]))
        grad_outs = []
        for seq, head, lanes in chains:
            out = raw[0, seq, :, lanes]
            rate = lax.rsqrt(jnp.mean(out * out, axis=-1, keepdims=True) + EPS)
            unit = out * rate
            gate = projected[3, 0, seq, :, lanes].astype(F32)
            gate_sig = sigmoid(gate)
            gate_act = gate * gate_sig
            arriving = grad_gated[0, seq, :, lanes].astype(F32)
            gain_sum[...] += fold_rows(arriving * unit * gate_act)
            arriving = arriving * gain[...]
            grad_projected[3, 0, seq, :, lanes] = narrow(arriving * unit * slope(gate, gate_sig))
            arriving = arriving * gate_act
            grad_outs.append(
                narrow(rate * (arriving - unit * jnp.mean(arriving * unit, axis=-1, keepdims=True)))
            )
        nows = [states[0, seq, :, lanes] for seq, head, lanes in chains]
        laters = [grad_state[seq, head] for seq, head, lanes in chains]
        updates = [adjusted[0, seq, :, lanes] for seq, head, lanes in chains]
        highs = [narrow(now) for now in nows]
        reads = [
            dot_nn(
                key, jnp.concatenate([high, narrow(now - high.astype(F32)), narrow(later)], axis=1)
            )
            for key, high, now, later in zip(keys, highs, nows, laters)
        ]
        scores_t = [
            narrow(jnp.where(row <= col, dot_nt(key, query), 0.0)) for key, query in zip(keys, queries)
        ]
        grams = [dot_nt(key, key) for key in keys]
        grad_updates = [
            read[:, 2 * HEAD_DIM :] + dot_nn(score, grad_out)
            for read, score, grad_out in zip(reads, scores_t, grad_outs)
        ]
        grad_targets = [
            grad_update + dot_nn(inverse[0, seq, :, lanes], grad_update)
            for grad_update, (seq, head, lanes) in zip(grad_updates, chains)
        ]
        grad_remains = [beta * grad_target for beta, grad_target in zip(betas, grad_targets)]
        rounded = [narrow(grad_remain) for grad_remain in grad_remains]
        earlier = [
            later
            + dot_tn(
                jnp.concatenate([query, key], axis=0), jnp.concatenate([grad_out, -grad_remain], axis=0)
            )
            for later, query, key, grad_out, grad_remain in zip(laters, queries, keys, grad_outs, rounded)
        ]
        for (seq, head, lanes), value in zip(chains, earlier):
            grad_state[seq, head] = value
        lowers = [
            dot_nt(jnp.concatenate([grad_out, narrow(grad_target)], axis=0), update)
            for grad_out, grad_target, update in zip(grad_outs, grad_targets, updates)
        ]
        uppers = [
            dot_nt(update, jnp.concatenate([grad_out, grad_remain], axis=0))
            for update, grad_out, grad_remain in zip(updates, grad_outs, rounded)
        ]
        by_states = [
            dot_nt(jnp.concatenate([grad_out, grad_remain], axis=0), high)
            for grad_out, grad_remain, high in zip(grad_outs, rounded, highs)
        ]
        by_laters = [dot_nt(update, later) for update, later in zip(updates, laters)]
        by_keys = []
        for index, (seq, head, lanes) in enumerate(chains):
            lower, upper, read, beta = lowers[index], uppers[index], reads[index], betas[index]
            remain = values[index].astype(F32) - (
                read[:, :HEAD_DIM] + read[:, HEAD_DIM : 2 * HEAD_DIM]
            )
            grad_lower = jnp.where(row > col, lower[CHUNK:], 0.0)
            grad_beta = jnp.sum(
                grad_targets[index] * remain - grad_lower * grams[index], axis=-1, keepdims=True
            )
            grad_logits[0, seq, :, head : head + 1] = grad_beta * beta * (1.0 - beta)
            grad_gram = -beta * grad_lower - jnp.where(row < col, upper[:, CHUNK:], 0.0)
            grad_scores = jnp.where(row >= col, lower[:CHUNK], 0.0)
            by_keys.append(
                dot_nn(
                    jnp.concatenate([narrow(grad_scores), narrow(grad_gram)], axis=0), keys[index]
                )
            )
        by_queries = [
            dot_nn(jnp.where(row <= col, upper[:, :CHUNK], 0.0), query)
            for upper, query in zip(uppers, queries)
        ]
        for index, (seq, head, lanes) in enumerate(chains):
            by_key, by_state, scale = by_keys[index], by_states[index], scales[index]
            grad_query = by_key[:CHUNK] + by_state[:CHUNK]
            grad_key = by_key[CHUNK:] - by_state[CHUNK:] + by_queries[index] + by_laters[index]
            along = jnp.sum(lengths[index] * grad_key, axis=-1, keepdims=True)
            grad_key = scale * (grad_key - lengths[index] * (scale * scale * along))
            for position, grad_act in enumerate((grad_query, grad_key, grad_remains[index])):
                trailing[seq, position, pl.ds(0, CHUNK), lanes] = grad_act * slopes[index][position]
        for seq, head, lanes in chains:
            for position in range(3):
                kept = trailing[seq, position, pl.ds(0, CHUNK), lanes]
                total = None
                for offset in range(4):
                    taps_sum[position, offset, :, lanes] += fold_rows(
                        kept * padded[seq, position, pl.ds(5 + offset, CHUNK), lanes]
                    )
                    term = taps[position, offset : offset + 1, lanes] * trailing[
                        seq, position, pl.ds(3 - offset, CHUNK), lanes
                    ]
                    total = term if total is None else total + term
                grad_projected[position, 0, seq, :, lanes] = narrow(total)

    @pl.when(step == last)
    def _():
        grad_state_out[...] = grad_state[...]
        after_out[...] = trailing[:, :, pl.ds(0, 8), :]
        grad_taps[...] = jnp.sum(taps_sum[...], axis=2)
        grad_gain[...] = jnp.sum(gain_sum[...], axis=0, keepdims=True)


def specs_for(shape, at):
    _, seqs, _, channels = shape

    def rows(width=channels):
        return pl.BlockSpec((1, seqs, CHUNK, width), lambda t, o: (o[0, at(t)], 0, o[1, at(t)], 0))

    planes = pl.BlockSpec(
        (4, 1, seqs, CHUNK, channels), lambda t, o: (0, o[0, at(t)], 0, o[1, at(t)], 0)
    )

    def whole(*shape):
        return pl.BlockSpec(shape, lambda t, o: (0,) * len(shape))

    return rows, planes, whole


def delta_forward(order, projected, logits, taps, gain, state_in, halo_in):
    shape = projected.shape[1:]
    seqs, channels = shape[1], shape[3]
    heads = channels // HEAD_DIM
    steps = shape[0] * shape[2] // CHUNK
    rows, planes, whole = specs_for(shape, lambda t: t)
    return pl.pallas_call(
        forward_kernel,
        out_shape=[
            jax.ShapeDtypeStruct(shape, dtype) for dtype in (BF16, F32, BF16, F32, BF16)
        ]
        + [jax.ShapeDtypeStruct((seqs, heads, HEAD_DIM, HEAD_DIM), F32)],
        grid_spec=pltpu.PrefetchScalarGridSpec(
            num_scalar_prefetch=1,
            grid=(steps,),
            in_specs=[
                planes,
                rows(heads),
                whole(3, 4, channels),
                whole(1, HEAD_DIM),
                whole(seqs, heads, HEAD_DIM, HEAD_DIM),
                whole(seqs, 3, 8, channels),
            ],
            out_specs=[rows() for _ in range(5)] + [whole(seqs, heads, HEAD_DIM, HEAD_DIM)],
            scratch_shapes=[
                pltpu.VMEM((seqs, heads, HEAD_DIM, HEAD_DIM), F32),
                pltpu.VMEM((seqs, 3, CHUNK + 8, channels), F32),
            ],
        ),
        compiler_params=pltpu.CompilerParams(
            dimension_semantics=("arbitrary",), vmem_limit_bytes=56 * 2**20
        ),
        cost_estimate=BRIEF,
        name="delta_forward",
    )(order, projected, logits, taps, gain, state_in, halo_in)


def delta_backward(
    order, projected, logits, taps, gain, halo_in, grad_gated, saved, grad_state_in, after_in
):
    shape = projected.shape[1:]
    seqs, channels = shape[1], shape[3]
    heads = channels // HEAD_DIM
    steps = shape[0] * shape[2] // CHUNK
    rows, planes, whole = specs_for(shape, lambda t: steps - 1 - t)
    part = CHUNK // 8

    def at_before(t, o):
        place = jnp.maximum(steps - 2 - t, 0)
        return (0, o[0, place], 0, o[1, place] * part + part - 1, 0)

    state_block = whole(seqs, heads, HEAD_DIM, HEAD_DIM)
    edge_block = whole(seqs, 3, 8, channels)
    return pl.pallas_call(
        backward_kernel,
        out_shape=[
            jax.ShapeDtypeStruct((4,) + shape, BF16),
            jax.ShapeDtypeStruct(shape[:3] + (heads,), F32),
            jax.ShapeDtypeStruct((3, 4, channels), F32),
            jax.ShapeDtypeStruct((1, HEAD_DIM), F32),
            jax.ShapeDtypeStruct((seqs, heads, HEAD_DIM, HEAD_DIM), F32),
            jax.ShapeDtypeStruct((seqs, 3, 8, channels), F32),
        ],
        grid_spec=pltpu.PrefetchScalarGridSpec(
            num_scalar_prefetch=1,
            grid=(steps,),
            in_specs=[
                planes,
                pl.BlockSpec((3, 1, seqs, 8, channels), at_before),
                rows(heads),
                whole(3, 4, channels),
                whole(1, HEAD_DIM),
                edge_block,
            ]
            + [rows() for _ in range(5)]
            + [state_block, edge_block],
            out_specs=[
                planes,
                rows(heads),
                whole(3, 4, channels),
                whole(1, HEAD_DIM),
                state_block,
                edge_block,
            ],
            scratch_shapes=[
                pltpu.VMEM((seqs, heads, HEAD_DIM, HEAD_DIM), F32),
                pltpu.VMEM((seqs, 3, CHUNK + 8, channels), F32),
                pltpu.VMEM((seqs, 3, CHUNK + 8, channels), F32),
                pltpu.VMEM((3, 4, 8, channels), F32),
                pltpu.VMEM((8, HEAD_DIM), F32),
            ],
        ),
        compiler_params=pltpu.CompilerParams(
            dimension_semantics=("arbitrary",), vmem_limit_bytes=60 * 2**20
        ),
        cost_estimate=BRIEF,
        name="delta_backward",
    )(
        order,
        projected,
        projected,
        logits,
        taps,
        gain,
        halo_in,
        grad_gated,
        *saved,
        grad_state_in,
        after_in,
    )


def weight_kernel(left_count, right_count, planes, deps, order, *refs):
    lefts, rights = refs[: 4 * left_count], refs[4 * left_count : 4 * left_count + right_count]
    outs, turned = refs[4 * left_count + right_count + deps : -1], refs[-1]
    rows, columns = lefts[0].shape

    @pl.when(pl.program_id(0) == 0)
    def _():
        for piece in range(left_count):
            for outer in range(4):
                turned[pl.ds(outer * columns, columns), pl.ds(piece * rows, rows)] = lefts[
                    4 * piece + outer
                ][...].T

    total = None
    size = turned.shape[1] // right_count
    for piece in range(right_count):
        right = rights[piece][0] if planes else rights[piece][...]
        term = lax.dot_general(
            turned[:, pl.ds(piece * size, size)],
            right,
            (((1,), (0,)), ((), ())),
            preferred_element_type=F32,
        )
        total = term if total is None else total + term
    total = narrow(total)
    for plane, out in enumerate(outs):

        @pl.when(pl.program_id(0) == plane)
        def _():
            for outer in range(4):
                out[outer] = total[outer * columns : (outer + 1) * columns]


def weight_products(order, lefts, rights, deps=()):
    rows, width = lefts[0].shape
    all_rows = rows * len(lefts)
    columns = width // 8
    planes, right_rows, size = rights[0].shape

    def pick(outer):
        return lambda n, order: (0, order[outer])

    return pl.pallas_call(
        functools.partial(weight_kernel, len(lefts), len(rights), planes, len(deps)),
        out_shape=[jax.ShapeDtypeStruct((4, columns, size), BF16)] * planes,
        grid_spec=pltpu.PrefetchScalarGridSpec(
            num_scalar_prefetch=1,
            grid=(planes,),
            in_specs=[
                pl.BlockSpec((rows, columns), pick(outer), pipeline_mode=pl.Buffered(1))
                for _ in lefts
                for outer in range(4)
            ]
            + [pl.BlockSpec((1, right_rows, size), lambda n, order: (n, 0, 0))] * len(rights)
            + [pl.BlockSpec(memory_space=pl.ANY)] * len(deps),
            out_specs=[pl.BlockSpec((4, columns, size), lambda n, order: (0, 0, 0))] * planes,
            scratch_shapes=[pltpu.VMEM((4 * columns, all_rows), BF16)],
        ),
        compiler_params=pltpu.CompilerParams(
            dimension_semantics=("arbitrary",), vmem_limit_bytes=60 * 2**20
        ),
        cost_estimate=BRIEF,
        name="weight_products",
    )(order, *[left for left in lefts for _ in range(4)], *rights, *deps)


def feed_kernel(blocks, deps, *refs):
    normed_refs, grad_refs = refs[:blocks], refs[blocks : 2 * blocks]
    w_up_hbm, w_down_hbm = refs[2 * blocks : 2 * blocks + 2]
    refs = refs[2 * blocks + 2 + deps :]
    hidden, gate_grad, out, back = refs[:4]
    w_up, w_down, normed_rows, grad_rows, row_sems, sems = refs[4:]
    step = pl.program_id(0)
    slot = step % 2
    weights = [
        pltpu.make_async_copy(w_up_hbm.at[0], w_up.at[0], sems.at[0]),
        pltpu.make_async_copy(w_up_hbm.at[1], w_up.at[1], sems.at[1]),
        pltpu.make_async_copy(w_down_hbm, w_down, sems.at[2]),
    ]

    def fetch(place, into):
        return [
            pltpu.make_async_copy(normed_refs[place], normed_rows.at[into], row_sems.at[0, into]),
            pltpu.make_async_copy(grad_refs[place], grad_rows.at[into], row_sems.at[1, into]),
        ]

    @pl.when(step == 0)
    def _():
        first = fetch(0, 0)
        first[0].start()
        weights[0].start()
        weights[1].start()
        first[1].start()
        weights[2].start()

    for here in range(1, blocks):

        @pl.when(step == here - 1)
        def _():
            for copy in fetch(here, here % 2):
                copy.start()

    arrived = fetch(0, slot)
    arrived[0].wait()

    @pl.when(step == 0)
    def _():
        weights[0].wait()

    normed = normed_rows[slot]
    gate = dot_nn(normed, w_up[0])

    @pl.when(step == 0)
    def _():
        weights[1].wait()

    up = dot_nn(normed, w_up[1])
    arrived[1].wait()

    @pl.when(step == 0)
    def _():
        weights[2].wait()

    grad_hidden = dot_nt(grad_rows[slot], w_down[...])
    sig = sigmoid(gate)
    act = gate * sig
    inner = narrow(act * up)
    gate_back = narrow(grad_hidden * up * slope(gate, sig))
    up_back = narrow(grad_hidden * act)
    hidden[...] = inner
    gate_grad[0] = gate_back
    gate_grad[1] = up_back
    out[...] = narrow(dot_nn(inner, w_down[...]))
    back[...] = narrow(dot_nt(gate_back, w_up[0]) + dot_nt(up_back, w_up[1]))


def feed_forward(normed, grads, w_up, w_down, deps=()):
    blocks = len(normed)
    rows, width = normed[0].shape
    size = w_down.shape[0]
    anywhere = pl.BlockSpec(memory_space=pl.ANY)
    wide = jax.ShapeDtypeStruct((rows * blocks, width), BF16)
    return pl.pallas_call(
        functools.partial(feed_kernel, blocks, len(deps)),
        out_shape=[
            jax.ShapeDtypeStruct((rows * blocks, size), BF16),
            jax.ShapeDtypeStruct((2, rows * blocks, size), BF16),
            wide,
            wide,
        ],
        grid=(blocks,),
        in_specs=[anywhere] * (2 * blocks + 2 + len(deps)),
        out_specs=[
            pl.BlockSpec((rows, size), lambda i: (i, 0)),
            pl.BlockSpec((2, rows, size), lambda i: (0, i, 0)),
            pl.BlockSpec((rows, width), lambda i: (i, 0)),
            pl.BlockSpec((rows, width), lambda i: (i, 0)),
        ],
        scratch_shapes=[
            pltpu.VMEM((2, width, size), BF16),
            pltpu.VMEM((size, width), BF16),
            pltpu.VMEM((2, rows, width), BF16),
            pltpu.VMEM((2, rows, width), BF16),
            pltpu.SemaphoreType.DMA((2, 2)),
            pltpu.SemaphoreType.DMA((3,)),
        ],
        compiler_params=pltpu.CompilerParams(
            dimension_semantics=("arbitrary",), vmem_limit_bytes=60 * 2**20
        ),
        cost_estimate=BRIEF,
        name="feed_forward",
    )(*normed, *grads, w_up, w_down, *deps)


def rows_kernel(blocks, planes, transposed, deps, *refs):
    row_refs, weight_hbm = refs[:blocks], refs[blocks]
    out, weight, now, row_sems, sems = refs[blocks + 1 + deps :]
    step = pl.program_id(0)
    slot = step % 2
    loads = [
        pltpu.make_async_copy(weight_hbm.at[plane], weight.at[plane], sems.at[plane])
        for plane in range(planes)
    ]

    def fetch(place, into):
        return pltpu.make_async_copy(row_refs[place], now.at[into], row_sems.at[into])

    @pl.when(step == 0)
    def _():
        fetch(0, 0).start()
        for load in loads:
            load.start()

    for here in range(1, blocks):

        @pl.when(step == here - 1)
        def _():
            fetch(here, here % 2).start()

    fetch(0, slot).wait()
    value = now[slot]
    for plane in range(planes):

        @pl.when(step == 0)
        def _():
            loads[plane].wait()

        out[plane] = (dot_nt if transposed else dot_nn)(value, weight[plane]).astype(out.dtype)


def rows_product(blocks, weight, transposed, dtype, deps=()):
    rows, width = blocks[0].shape
    planes = weight.shape[0]
    size = weight.shape[1] if transposed else weight.shape[2]
    anywhere = pl.BlockSpec(memory_space=pl.ANY)
    count = len(blocks)
    return pl.pallas_call(
        functools.partial(rows_kernel, count, planes, transposed, len(deps)),
        out_shape=jax.ShapeDtypeStruct((planes, rows * count, size), dtype),
        grid=(count,),
        in_specs=[anywhere] * (count + 1 + len(deps)),
        out_specs=pl.BlockSpec((planes, rows, size), lambda i: (0, i, 0)),
        scratch_shapes=[
            pltpu.VMEM(weight.shape, BF16),
            pltpu.VMEM((2, rows, width), BF16),
            pltpu.SemaphoreType.DMA((2,)),
            pltpu.SemaphoreType.DMA((planes,)),
        ],
        compiler_params=pltpu.CompilerParams(
            dimension_semantics=("arbitrary",), vmem_limit_bytes=60 * 2**20
        ),
        cost_estimate=BRIEF,
        name="rows_product",
    )(*blocks, weight, *deps)


def input_kernel(planes, deps, *refs):
    grad, logit, weight_hbm, beta_weight = refs[:4]
    away, near, weight, sems = refs[4 + deps :]
    step = pl.program_id(0)
    loads = [
        pltpu.make_async_copy(weight_hbm.at[plane], weight.at[plane], sems.at[plane])
        for plane in range(planes)
    ]

    @pl.when(step == 0)
    def _():
        for load in loads:
            load.start()

    total = dot_nt(logit[...], beta_weight[...])
    for plane in range(planes):

        @pl.when(step == 0)
        def _():
            loads[plane].wait()

        total = total + dot_nt(grad[plane], weight[plane])
    total = narrow(total)
    half = pl.num_programs(0) // 2

    @pl.when(step < half)
    def _():
        away[...] = total

    @pl.when(step >= half)
    def _():
        near[...] = total


def input_product(grad, logit, weight, beta_weight, block, deps=()):
    planes, rows, size = grad.shape
    width = weight.shape[1]
    count = rows // block
    half = count // 2
    place = lambda i: (i + half) % count
    anywhere = pl.BlockSpec(memory_space=pl.ANY)
    return pl.pallas_call(
        functools.partial(input_kernel, planes, len(deps)),
        out_shape=[jax.ShapeDtypeStruct((rows // 2, width), BF16)] * 2,
        grid=(count,),
        in_specs=[
            pl.BlockSpec((planes, block, size), lambda i: (0, place(i), 0)),
            pl.BlockSpec((block, logit.shape[1]), lambda i: (place(i), 0)),
            anywhere,
            pl.BlockSpec(beta_weight.shape, lambda i: (0, 0)),
        ]
        + [anywhere] * len(deps),
        out_specs=[
            pl.BlockSpec((block, width), lambda i: (jnp.minimum(i, half - 1), 0)),
            pl.BlockSpec((block, width), lambda i: (jnp.maximum(i - half, 0), 0)),
        ],
        scratch_shapes=[pltpu.VMEM(weight.shape, BF16), pltpu.SemaphoreType.DMA((planes,))],
        compiler_params=pltpu.CompilerParams(
            dimension_semantics=("arbitrary",), vmem_limit_bytes=60 * 2**20
        ),
        cost_estimate=BRIEF,
        name="input_product",
    )(grad, logit, weight, beta_weight, *deps)


def rms_scale(signal, gain):
    return signal * lax.rsqrt(jnp.mean(signal * signal, axis=-1, keepdims=True) + EPS) * gain


def rms_back(signal, gain, grad):
    rate = lax.rsqrt(jnp.mean(signal * signal, axis=-1, keepdims=True) + EPS)
    unit = signal * rate
    scaled = grad * gain
    grad_signal = rate * (scaled - unit * jnp.mean(scaled * unit, axis=-1, keepdims=True))
    return grad_signal, jnp.sum(grad * unit, axis=0)


def tie(*values):
    return lax.optimization_barrier(values)


def hold(value, *others):
    return tie(value, *others)[0]


def swap(value, axis, distance):
    size = lax.axis_size(axis)
    return lax.ppermute(value, axis, [(place, place ^ distance) for place in range(size)])


def sum_over(value, axis):
    distance = 1
    while distance < lax.axis_size(axis):
        value = value + swap(value, axis, distance)
        distance *= 2
    return value


def own_scale(group_ids, group_weight, seqs_here, own_seq):
    group_range = jnp.arange(GROUPS, dtype=jnp.int32)
    member = (group_ids[:, None] == group_range[None, :]).astype(jnp.int32)
    counts = sum_over(jnp.sum(member, axis=0) * LEN, "dp").astype(F32)
    member_float = member.astype(F32)
    seq_weight = jnp.sum(member_float * group_weight.astype(F32)[None, :], axis=1)
    seq_count = jnp.sum(member_float * counts[None, :], axis=1)
    total_tokens = LEN * seqs_here * lax.axis_size("dp")
    seq_scale = seq_weight * total_tokens / (GROUPS * seq_count)
    return jnp.sum(jnp.where(jnp.arange(seqs_here) == own_seq, seq_scale, 0.0))


def sum_small(grad_beta, grad_taps, gain_one, gain_two, gain_heads):
    beta_size, taps_size, width = grad_beta.size, grad_taps.size, gain_one.size
    small = sum_over(
        jnp.concatenate(
            [grad_beta.reshape(-1), grad_taps.reshape(-1), gain_one, gain_two, gain_heads]
        ),
        "dp",
    )
    gains = sum_over(small[beta_size + taps_size :], "head")
    return (
        small[:beta_size].reshape(grad_beta.shape),
        small[beta_size : beta_size + taps_size].reshape(grad_taps.shape),
        gains[:width],
        gains[width : 2 * width],
        gains[2 * width :],
    )


def plain_body(
    tokens,
    norm_gain,
    w_proj,
    w_beta,
    conv_weight,
    head_gain,
    w_out,
    ffn_gain,
    w_ffn,
    w_down,
    group_ids,
    group_weight,
    cotangent,
):
    rows_here = tokens.shape[0]
    head_pos = lax.axis_index("head")
    seqs = rows_here * lax.axis_size("head") // LEN
    channels = w_proj.shape[2]
    heads = channels // HEAD_DIM
    gain_one, gain_two = norm_gain.astype(F32), ffn_gain.astype(F32)
    gain_heads, taps = head_gain.astype(F32)[None], conv_weight.astype(F32)

    def gather(rows):
        return lax.all_gather(narrow(rows), "head", axis=0, tiled=True)

    def scatter(partial):
        return lax.psum_scatter(narrow(partial), "head", scatter_dimension=0, tiled=True).astype(F32)

    def scatter_weight(product, dim):
        return lax.psum_scatter(narrow(product), "dp", scatter_dimension=dim, tiled=True).astype(F32)

    def product(form, left, right):
        return jnp.einsum(form, left, right, preferred_element_type=F32)

    x_here = tokens.astype(F32)
    scale = own_scale(group_ids, group_weight, seqs, (head_pos * rows_here) // LEN)
    upstream = cotangent.astype(F32) * scale
    normed = gather(rms_scale(x_here, gain_one))
    grad_ffn = gather(upstream)
    steps = LEN // CHUNK
    order = jnp.stack([jnp.zeros(steps, jnp.int32), jnp.arange(steps, dtype=jnp.int32)])

    def by_seq(rows):
        return rows.reshape(rows.shape[:-2] + (1, seqs, LEN, rows.shape[-1]))

    def flat(rows):
        return rows.reshape(rows.shape[:-4] + (seqs * LEN, rows.shape[-1]))

    projected = by_seq(product("td,fdk->ftk", normed, w_proj))
    logits = by_seq(product("td,dh->th", normed, w_beta))
    state = jnp.zeros((seqs, heads, HEAD_DIM, HEAD_DIM), F32)
    halo = jnp.zeros((seqs, 3, 8, channels), F32)
    gated, *saved, _ = delta_forward(order, projected, logits, taps, gain_heads, state, halo)
    gated = flat(gated)
    middle = x_here + scatter(product("tk,kd->td", gated, w_out))
    normed_two = gather(rms_scale(middle, gain_two))
    gate_up = product("td,fdk->ftk", normed_two, w_ffn)
    grad_hidden = product("td,fd->tf", grad_ffn, w_down)
    sig = sigmoid(gate_up[0])
    act = gate_up[0] * sig
    hidden = narrow(act * gate_up[1])
    gate_grad = jnp.stack(
        [narrow(grad_hidden * gate_up[1] * slope(gate_up[0], sig)), narrow(grad_hidden * act)]
    )
    mixed_out = narrow(middle + scatter(product("tk,kd->td", hidden, w_down)))
    through, gain_two_sum = rms_back(
        middle, gain_two, scatter(product("ftk,fdk->td", gate_grad, w_ffn))
    )
    grad_middle = upstream + through
    grad_mixer = gather(grad_middle)
    back, logit_back, taps_back, gain_back, _, _ = delta_backward(
        order,
        projected,
        logits,
        taps,
        gain_heads,
        halo,
        by_seq(product("td,kd->tk", grad_mixer, w_out)),
        saved,
        state,
        halo,
    )
    back, logit_back = flat(back), narrow(flat(logit_back))
    grad_normed = scatter(
        product("ftk,fdk->td", back, w_proj) + product("th,dh->td", logit_back, w_beta)
    )
    through, gain_one_sum = rms_back(x_here, gain_one, grad_normed)
    beta, conv, gain_one_sum, gain_two_sum, gain_back = sum_small(
        product("td,th->dh", normed, logit_back), taps_back, gain_one_sum, gain_two_sum, gain_back[0]
    )
    return (
        mixed_out,
        grad_middle + through,
        gain_one_sum,
        scatter_weight(product("td,ftk->fdk", normed, back), 1),
        beta,
        conv,
        gain_back,
        scatter_weight(product("tk,td->kd", gated, grad_mixer), 1),
        gain_two_sum,
        scatter_weight(product("td,ftk->fdk", normed_two, gate_grad), 1),
        scatter_weight(product("tf,td->fd", hidden, grad_ffn), 1),
    )


def pair_sum(away, near):
    return near.astype(F32) + swap(away, "head", 1).astype(F32)


def own_half(total):
    return total[: total.shape[0] // 2]


def far_half(total):
    return swap(narrow(total[total.shape[0] // 2 :]), "head", 2)


def paired_body(
    tokens,
    norm_gain,
    w_proj,
    w_beta,
    conv_weight,
    head_gain,
    w_out,
    ffn_gain,
    w_ffn,
    w_down,
    group_ids,
    group_weight,
    cotangent,
):
    rows_here, width = tokens.shape
    head_pos = lax.axis_index("head")
    core = head_pos % 2
    place = lax.axis_index("dp")
    outer, inner = place // 2, place % 2
    seqs = 2
    channels = w_proj.shape[2]
    heads = channels // HEAD_DIM
    half = rows_here // 2
    gain_one, gain_two = norm_gain.astype(F32), ffn_gain.astype(F32)
    gain_heads, taps = head_gain.astype(F32)[None], conv_weight.astype(F32)

    def deal(rows):
        first, second = rows[:half], rows[half:]
        other = swap(jnp.where(core == 0, second, first), "head", 1)
        return jnp.where(core == 0, first, other), jnp.where(core == 0, other, second)

    def undeal(early, late):
        other = swap(jnp.where(core == 0, late, early), "head", 1)
        return jnp.concatenate(
            [jnp.where(core == 0, early, other), jnp.where(core == 0, other, late)], axis=0
        )

    def product(left, right):
        return jnp.dot(left, right, preferred_element_type=F32)

    split = half // CHUNK
    step_range = jnp.arange(2 * split, dtype=jnp.int32)
    order = jnp.stack([(step_range // split) ^ core, step_range % split])

    def by_seq(rows):
        return rows.reshape(rows.shape[:-2] + (2, seqs, half, rows.shape[-1]))

    def flat(rows):
        return rows.reshape(rows.shape[:-4] + (2 * seqs * half, rows.shape[-1]))

    near_order = 2 * (outer ^ jnp.array([0, 2, 1, 3], dtype=jnp.int32)) + inner
    away_order = near_order ^ 1

    def far_of(rows):
        return swap(rows, "head", 2)

    def blocks(rows, far):
        return [rows, far, swap(rows, "head", 1), swap(far, "head", 1)]

    def logits_of(normed):
        return jnp.concatenate([product(block, w_beta) for block in normed], axis=0)

    def mixer_out(gated):
        count = gated.shape[0] // 2
        return pair_sum(narrow(product(gated[count:], w_out)), product(gated[:count], w_out))

    def send(products):
        return [swap(value, "dp", 1) for value in products]

    def halve(kept, away):
        return swap(narrow(kept[2:].astype(F32) + away[2:].astype(F32)), "dp", 2)

    def halve_again(kept, away, first):
        return swap(
            narrow(kept[1].astype(F32) + away[1].astype(F32) + first[1].astype(F32)), "dp", 4
        )

    def finish(kept, away, first, second):
        return (
            kept[0].astype(F32) + away[0].astype(F32) + first[0].astype(F32) + second.astype(F32)
        )

    x_a, x_b = [part.astype(F32) for part in deal(tokens)]
    rows_a, rows_b = narrow(rms_scale(x_a, gain_one)), narrow(rms_scale(x_b, gain_one))
    far_a = far_of(rows_a)
    normed_a = blocks(rows_a, far_a)
    scale = own_scale(group_ids, group_weight, seqs, head_pos // 2)
    up_a, up_b = [part.astype(F32) * scale for part in deal(cotangent)]
    up_rows_a, up_rows_b = narrow(up_a), narrow(up_b)
    far_b = far_of(rows_b)
    up_far_a = far_of(hold(up_rows_a, far_a))

    state = jnp.zeros((seqs, heads, HEAD_DIM, HEAD_DIM), F32)
    halo_a = jnp.zeros((seqs, 3, 8, channels), F32)
    projected_a = by_seq(rows_product(normed_a, w_proj, False, F32))
    logits_a = by_seq(logits_of(normed_a))
    gated_a, *saved_a, state_a = delta_forward(
        order, projected_a, logits_a, taps, gain_heads, state, halo_a
    )
    gated_a = flat(gated_a)
    halo_b = lax.dynamic_slice(
        projected_a, (0, 1 - core, 0, half - 8, 0), (3, 1, seqs, 8, channels)
    )[:, 0].transpose(1, 0, 2, 3)
    gated_a, far_b, up_far_a = lax.optimization_barrier((gated_a, far_b, up_far_a))
    mixer_a = mixer_out(gated_a)
    mixer_far_a = far_half(mixer_a)
    up_far_b = far_of(hold(up_rows_b, mixer_a))

    normed_b = blocks(rows_b, far_b)
    grad_ffn_a = blocks(up_rows_a, up_far_a)
    projected_b = by_seq(rows_product(hold(normed_b, mixer_a), w_proj, False, F32))
    logits_b = by_seq(logits_of(normed_b))
    gated_b, *saved_b, _ = delta_forward(
        order, projected_b, logits_b, taps, gain_heads, state_a, halo_b
    )
    gated_b = flat(gated_b)
    gated_b, mixer_far_a, up_far_b = lax.optimization_barrier((gated_b, mixer_far_a, up_far_b))
    middle_a = x_a + own_half(mixer_a) + mixer_far_a.astype(F32)
    rows_a = narrow(rms_scale(middle_a, gain_two))
    two_far_a = far_of(rows_a)
    mixer_b = mixer_out(hold(gated_b, rows_a))
    mixer_far_b = far_half(mixer_b)
    two_a = blocks(rows_a, hold(two_far_a, mixer_b))
    grad_ffn_b = blocks(up_rows_b, up_far_b)

    def feed(normed, grads):
        return feed_forward(normed, grads, w_ffn, w_down)

    away_a = feed(two_a[2:], grad_ffn_a[2:])
    away_a, mixer_far_b = lax.optimization_barrier((away_a, mixer_far_b))
    middle_b = x_b + own_half(mixer_b) + mixer_far_b.astype(F32)
    rows_b = narrow(rms_scale(middle_b, gain_two))
    two_far_b = far_of(rows_b)
    near_a = feed(hold(two_a[:2], rows_b), grad_ffn_a[:2])
    near_a, two_far_b = lax.optimization_barrier((near_a, two_far_b))
    back_a = pair_sum(away_a[3], near_a[3])
    back_far_a = far_half(back_a)
    out_a = pair_sum(away_a[2], hold(near_a[2], back_a))
    out_far_a = far_half(out_a)
    two_b = blocks(rows_b, two_far_b)
    away_b = feed(hold(two_b[2:], back_a, out_a), grad_ffn_b[2:])
    away_b, back_far_a = lax.optimization_barrier((away_b, back_far_a))
    through, gain_two_a = rms_back(middle_a, gain_two, own_half(back_a) + back_far_a.astype(F32))
    grad_middle_a = up_a + through
    mix_rows_a = narrow(grad_middle_a)
    mix_far_a = far_of(mix_rows_a)
    near_b = feed(hold(two_b[:2], mix_rows_a), grad_ffn_b[:2])
    near_b, mix_far_a, out_far_a = lax.optimization_barrier((near_b, mix_far_a, out_far_a))
    back_b = pair_sum(away_b[3], near_b[3])
    back_far_b = far_half(back_b)

    down_left = grad_ffn_a + grad_ffn_b
    down_right = [part[0][None] for part in (near_a, away_a, near_b, away_b)]
    up_left = two_a + two_b
    up_right = [part[1] for part in (near_a, away_a, near_b, away_b)]
    down_sent = weight_products(hold(away_order, back_b), down_left, down_right)
    (down_away,) = send(down_sent)
    up_sent = weight_products(hold(away_order, *down_sent), up_left, up_right)
    up_sent, back_far_b = lax.optimization_barrier((up_sent, back_far_b))
    up_away_0, up_away_1 = send(up_sent)
    through, gain_two_b = rms_back(middle_b, gain_two, own_half(back_b) + back_far_b.astype(F32))
    grad_middle_b = up_b + through
    mix_rows_b = narrow(grad_middle_b)
    mix_far_b = far_of(mix_rows_b)
    out_b = pair_sum(away_b[2], hold(near_b[2], mix_rows_b))
    out_far_b = far_half(out_b)
    (down_kept,) = weight_products(hold(near_order, mix_rows_b, out_b), down_left, down_right)
    w_out_plane = w_out[None]
    grad_mixer_a = blocks(mix_rows_a, mix_far_a)
    grad_gated_a = rows_product(hold(grad_mixer_a, down_kept), w_out_plane, True, F32)[0]
    grad_gated_a, mix_far_b = lax.optimization_barrier((grad_gated_a, mix_far_b))
    grad_mixer_b = blocks(mix_rows_b, mix_far_b)
    grad_gated_b = rows_product(hold(grad_mixer_b, grad_gated_a), w_out_plane, True, F32)[0]
    grad_gated_b, down_away = lax.optimization_barrier((grad_gated_b, down_away))
    down_first = halve(down_kept, down_away)

    zero_state = jnp.zeros((seqs, heads, HEAD_DIM, HEAD_DIM), F32)
    zero_after = jnp.zeros((seqs, 3, 8, channels), F32)
    late = delta_backward(
        order,
        projected_b,
        logits_b,
        taps,
        gain_heads,
        halo_b,
        by_seq(grad_gated_b),
        saved_b,
        zero_state,
        zero_after,
    )
    late, down_first = lax.optimization_barrier((late, down_first))
    proj_b, logit_b, taps_b, gain_heads_b, grad_state, after = late
    down_second = halve_again(down_kept, down_away, down_first)
    up_kept_0, up_kept_1 = weight_products(hold(near_order, grad_state), up_left, up_right)
    up_kept_0, up_kept_1, up_away_0 = lax.optimization_barrier((up_kept_0, up_kept_1, up_away_0))
    up_first_0 = halve(up_kept_0, up_away_0)
    out_left, out_right = grad_mixer_a + grad_mixer_b, [gated_a[None], gated_b[None]]
    (out_sent,) = weight_products(hold(away_order, up_kept_0), out_left, out_right)
    (out_away,) = send([out_sent])
    early = delta_backward(
        order,
        projected_a,
        logits_a,
        taps,
        gain_heads,
        halo_a,
        by_seq(grad_gated_a),
        saved_a,
        hold(grad_state, out_sent),
        after,
    )
    early, up_first_0, down_second = lax.optimization_barrier((early, up_first_0, down_second))
    proj_a, logit_a, taps_a, gain_heads_a, _, _ = early
    proj_a, proj_b = flat(proj_a), flat(proj_b)
    logit_a, logit_b = narrow(flat(logit_a)), narrow(flat(logit_b))
    up_second_0 = halve_again(up_kept_0, up_away_0, up_first_0)
    proj_left, proj_right = normed_a + normed_b, [proj_a, proj_b]
    proj_sent = weight_products(away_order, proj_left, proj_right)
    proj_sent, up_away_1, proj_a = tie(proj_sent, up_away_1, proj_a)
    proj_away = send(proj_sent)
    up_first_1 = halve(up_kept_1, up_away_1)
    inputs_a = input_product(proj_a, logit_a, w_proj, w_beta, half)
    inputs_a, out_away, proj_b = tie(inputs_a, out_away, proj_b)
    inputs_b = input_product(proj_b, logit_b, w_proj, w_beta, half)
    inputs_a, inputs_b, proj_away[0] = tie(inputs_a, inputs_b, proj_away[0])
    in_a = pair_sum(*inputs_a)
    in_b = pair_sum(*inputs_b)
    in_a, in_b, near_order = tie(in_a, in_b, near_order)
    in_far_a = far_half(in_a)
    in_far_b = far_half(in_b)
    proj_kept = weight_products(near_order, proj_left, proj_right)
    proj_kept, up_first_1, proj_away[1], near_order = tie(
        proj_kept, up_first_1, proj_away[1], near_order
    )
    proj_first = [halve(kept, away) for kept, away in zip(proj_kept[:2], proj_away[:2])]
    (out_kept,) = weight_products(near_order, out_left, out_right)
    up_second_1 = halve_again(up_kept_1, up_away_1, up_first_1)
    out_kept, proj_away[2], out_a, out_b = tie(out_kept, proj_away[2], out_a, out_b)
    proj_first.append(halve(proj_kept[2], proj_away[2]))
    out_first = halve(out_kept, out_away)
    proj_second = [
        halve_again(kept, away, first)
        for kept, away, first in zip(proj_kept[:2], proj_away[:2], proj_first[:2])
    ]
    out_second = halve_again(out_kept, out_away, out_first)
    proj_first.append(halve(proj_kept[3], proj_away[3]))
    for index in (2, 3):
        proj_second.append(
            halve_again(proj_kept[index], proj_away[index], proj_first[index])
        )

    mixed_out = undeal(
        narrow(middle_a + own_half(out_a) + out_far_a.astype(F32)),
        narrow(middle_b + own_half(out_b) + out_far_b.astype(F32)),
    )
    through_b, gain_one_b = rms_back(x_b, gain_one, own_half(in_b) + in_far_b.astype(F32))
    through_a, gain_one_a = rms_back(x_a, gain_one, own_half(in_a) + in_far_a.astype(F32))
    grad_tokens = undeal(grad_middle_a + through_a, grad_middle_b + through_b)
    grad_beta = 0.0
    for normed, logit in ((normed_a, logit_a), (normed_b, logit_b)):
        for index, block in enumerate(normed):
            grad_beta = grad_beta + jnp.einsum(
                "td,th->dh",
                block,
                logit[index * half : (index + 1) * half],
                preferred_element_type=F32,
            )
    beta, conv, gain_one_sum, gain_two_sum, gain_heads_sum = sum_small(
        grad_beta,
        taps_a + taps_b,
        gain_one_a + gain_one_b,
        gain_two_a + gain_two_b,
        (gain_heads_a + gain_heads_b)[0],
    )
    return (
        mixed_out,
        grad_tokens,
        gain_one_sum,
        jnp.stack(
            [finish(*parts) for parts in zip(proj_kept, proj_away, proj_first, proj_second)]
        ),
        beta,
        conv,
        gain_heads_sum,
        finish(out_kept, out_away, out_first, out_second).T,
        gain_two_sum,
        jnp.stack(
            [
                finish(up_kept_0, up_away_0, up_first_0, up_second_0),
                finish(up_kept_1, up_away_1, up_first_1, up_second_1),
            ]
        ),
        finish(down_kept, down_away, down_first, down_second).T,
    )


def body(*args):
    rows_here, channels = args[0].shape[0], args[2].shape[2]
    paired = (
        lax.axis_size("head") == 4
        and lax.axis_size("dp") == 8
        and rows_here * 2 == LEN
        and channels % HEAD_DIM == 0
    )
    return (paired_body if paired else plain_body)(*args)


def solution(mesh):
    placed = (
        P(("dp", "head"), None),
        P(),
        P(None, None, "head"),
        P(None, "head"),
        P(None, None, "head"),
        P(),
        P("head", None),
        P(),
        P(None, None, "head"),
        P("head", None),
        P("dp"),
        P(),
        P(("dp", "head"), None),
    )
    return jax.shard_map(
        body,
        mesh=mesh,
        in_specs=placed,
        out_specs=(
            P(("dp", "head"), None),
            P(("dp", "head"), None),
            P(),
            P(None, "dp", "head"),
            P(None, "head"),
            P(None, None, "head"),
            P(),
            P("head", "dp"),
            P(),
            P(None, "dp", "head"),
            P("head", "dp"),
        ),
        check_vma=False,
    )
```

```python
import functools

import jax
import jax.numpy as jnp
from jax import lax
from jax.experimental import pallas as pl
from jax.experimental.pallas import tpu as pltpu
from jax.sharding import PartitionSpec as P

HEAD_DIM = 128
CHUNK = 128
LEN = 1024
BACK_CHAINS = 4
GROUPS = 4
EPS = 1e-06
F32 = jnp.float32
BF16 = jnp.bfloat16
BRIEF = pl.CostEstimate(flops=10**9, bytes_accessed=10**6, transcendentals=0)


def narrow(value):
    return value.astype(BF16)


def dot_nn(left, right):
    return lax.dot_general(
        narrow(left), narrow(right), (((1,), (0,)), ((), ())), preferred_element_type=F32
    )


def dot_nt(left, right):
    return lax.dot_general(
        narrow(left), narrow(right), (((1,), (1,)), ((), ())), preferred_element_type=F32
    )


def dot_tn(left, right):
    return lax.dot_general(
        narrow(left), narrow(right), (((0,), (0,)), ((), ())), preferred_element_type=F32
    )


def sigmoid(value):
    return 1.0 / (1.0 + jnp.exp(-value))


def invert_lower(matrices, row, col):
    joined = row ^ col
    extras = [-jnp.where(joined == 1, below, 0.0) for below in matrices]
    size = 2
    while size < CHUNK:
        inside = (joined >= size) & (joined < 2 * size)
        corners = [jnp.where(inside, below, 0.0) for below in matrices]
        lefts = [corner + dot_nn(extra, corner) for extra, corner in zip(extras, corners)]
        extras = [extra - left - dot_nn(left, extra) for extra, left in zip(extras, lefts)]
        size *= 2
    rounded = [narrow(extra) for extra in extras]
    highs = [narrow(below) for below in matrices]
    lows = [narrow(below - high.astype(F32)) for below, high in zip(matrices, highs)]
    products = [
        dot_nn(jnp.concatenate([high, low], axis=1), jnp.concatenate([kept, kept], axis=0))
        for high, low, kept in zip(highs, lows, rounded)
    ]
    wides = [kept.astype(F32) for kept in rounded]
    residuals = [
        -(below + wide + product) for below, wide, product in zip(matrices, wides, products)
    ]
    return [
        wide + residual + dot_nn(kept, residual)
        for wide, residual, kept in zip(wides, residuals, rounded)
    ]


def activate_taps(padded, taps, position, seq, lanes):
    summed = None
    for offset in range(4):
        term = taps[position, offset : offset + 1, lanes] * padded[seq, position, pl.ds(5 + offset, CHUNK), lanes]
        summed = term if summed is None else summed + term
    return summed


def chains_of(seqs, heads):
    return [(seq, head, pl.ds(head * HEAD_DIM, HEAD_DIM)) for seq in range(seqs) for head in range(heads)]


def masks():
    row = lax.broadcasted_iota(jnp.int32, (CHUNK, CHUNK), 0)
    col = lax.broadcasted_iota(jnp.int32, (CHUNK, CHUNK), 1)
    return row, col


def forward_kernel(
    order,
    projected,
    logits,
    taps,
    gain,
    state_in,
    halo_in,
    gated,
    raw,
    inverse,
    states,
    adjusted,
    state_out,
    state,
    padded,
):
    step = pl.program_id(0)
    seqs, heads = state.shape[:2]
    chains = chains_of(seqs, heads)

    @pl.when(step == 0)
    def _():
        state[...] = state_in[...]
        padded[:, :, pl.ds(0, 8), :] = halo_in[...]

    @pl.when(step > 0)
    def _():
        padded[:, :, pl.ds(0, 8), :] = padded[:, :, pl.ds(CHUNK, 8), :]

    for seq in range(seqs):
        for position in range(3):
            padded[seq, position, pl.ds(8, CHUNK), :] = projected[position, 0, seq].astype(F32)
    row, col = masks()
    queries, keys, values, betas = [], [], [], []
    for seq, head, lanes in chains:
        acts = []
        for position in range(3):
            summed = activate_taps(padded, taps, position, seq, lanes)
            acts.append(summed * sigmoid(summed))
        scale = lax.rsqrt(jnp.sum(acts[1] * acts[1], axis=-1, keepdims=True) + EPS)
        queries.append(narrow(acts[0]))
        keys.append(narrow(acts[1] * scale))
        values.append(narrow(acts[2]))
        betas.append(sigmoid(logits[0, seq, :, head : head + 1]))
    belows = [jnp.where(row > col, beta * dot_nt(key, key), 0.0) for key, beta in zip(keys, betas)]
    scores = [
        narrow(jnp.where(row >= col, dot_nt(query, key), 0.0)) for query, key in zip(queries, keys)
    ]
    extras = [narrow(extra) for extra in invert_lower(belows, row, col)]
    nows = [state[seq, head] for seq, head, _ in chains]
    reads = []
    for query, key, now in zip(queries, keys, nows):
        high = narrow(now)
        low = narrow(now - high.astype(F32))
        read = dot_nn(jnp.concatenate([key, query], axis=0), jnp.concatenate([high, low], axis=1))
        reads.append(read[:, :HEAD_DIM] + read[:, HEAD_DIM:])
    targets = [
        beta * (value.astype(F32) - read[:CHUNK]) for beta, value, read in zip(betas, values, reads)
    ]
    updates = [narrow(target + dot_nn(extra, target)) for extra, target in zip(extras, targets)]
    outs = [
        read[CHUNK:] + dot_nn(score, update) for read, score, update in zip(reads, scores, updates)
    ]
    laters = [now + dot_tn(key, update) for now, key, update in zip(nows, keys, updates)]
    for index, (seq, head, lanes) in enumerate(chains):
        state[seq, head] = laters[index]
        raw[0, seq, :, lanes] = outs[index]
        inverse[0, seq, :, lanes] = extras[index].T
        states[0, seq, :, lanes] = nows[index]
        adjusted[0, seq, :, lanes] = updates[index]
        gate = projected[3, 0, seq, :, lanes].astype(F32)
        rate = lax.rsqrt(jnp.mean(outs[index] * outs[index], axis=-1, keepdims=True) + EPS)
        gated[0, seq, :, lanes] = narrow(outs[index] * rate * gain[...] * (gate * sigmoid(gate)))

    @pl.when(step == pl.num_programs(0) - 1)
    def _():
        state_out[...] = state[...]


def slope(value, sig):
    return sig * (1.0 + value * (1.0 - sig))


def fold_rows(value):
    return jnp.sum(value.reshape(CHUNK // 8, 8, value.shape[-1]), axis=0)


def backward_kernel(
    order,
    projected,
    before,
    logits,
    taps,
    gain,
    halo_in,
    grad_gated,
    raw,
    inverse,
    states,
    adjusted,
    grad_state_in,
    after_in,
    grad_projected,
    grad_logits,
    grad_taps,
    grad_gain,
    grad_state_out,
    after_out,
    grad_state,
    padded,
    trailing,
    taps_sum,
    gain_sum,
):
    step = pl.program_id(0)
    last = pl.num_programs(0) - 1
    seqs, heads = grad_state.shape[:2]

    @pl.when(step == 0)
    def _():
        taps_sum[...] = jnp.zeros_like(taps_sum)
        gain_sum[...] = jnp.zeros_like(gain_sum)
        grad_state[...] = grad_state_in[...]
        trailing[:, :, pl.ds(CHUNK, 8), :] = after_in[...]

    @pl.when(step > 0)
    def _():
        trailing[:, :, pl.ds(CHUNK, 8), :] = trailing[:, :, pl.ds(0, 8), :]

    @pl.when(step == last)
    def _():
        padded[:, :, pl.ds(0, 8), :] = halo_in[...]

    @pl.when(step < last)
    def _():
        for seq in range(seqs):
            for position in range(3):
                padded[seq, position, pl.ds(0, 8), :] = before[position, 0, seq].astype(F32)

    for seq in range(seqs):
        for position in range(3):
            padded[seq, position, pl.ds(8, CHUNK), :] = projected[position, 0, seq].astype(F32)
    row, col = masks()
    everything = chains_of(seqs, heads)
    for begin in range(0, len(everything), BACK_CHAINS):
        chains = everything[begin : begin + BACK_CHAINS]
        slopes, lengths, scales, queries, keys, values, betas = [], [], [], [], [], [], []
        for seq, head, lanes in chains:
            sums = [activate_taps(padded, taps, position, seq, lanes) for position in range(3)]
            sigs = [sigmoid(summed) for summed in sums]
            acts = [summed * sig for summed, sig in zip(sums, sigs)]
            slopes.append([slope(summed, sig) for summed, sig in zip(sums, sigs)])
            scale = lax.rsqrt(jnp.sum(acts[1] * acts[1], axis=-1, keepdims=True) + EPS)
            lengths.append(acts[1])
            scales.append(scale)
            queries.append(narrow(acts[0]))
            keys.append(narrow(acts[1] * scale))
            values.append(narrow(acts[2]))
            betas.append(sigmoid(logits[0, seq, :, head : head + 1]))
        grad_outs = []
        for seq, head, lanes in chains:
            out = raw[0, seq, :, lanes]
            rate = lax.rsqrt(jnp.mean(out * out, axis=-1, keepdims=True) + EPS)
            unit = out * rate
            gate = projected[3, 0, seq, :, lanes].astype(F32)
            gate_sig = sigmoid(gate)
            gate_act = gate * gate_sig
            arriving = grad_gated[0, seq, :, lanes].astype(F32)
            gain_sum[...] += fold_rows(arriving * unit * gate_act)
            arriving = arriving * gain[...]
            grad_projected[3, 0, seq, :, lanes] = narrow(arriving * unit * slope(gate, gate_sig))
            arriving = arriving * gate_act
            grad_outs.append(
                narrow(rate * (arriving - unit * jnp.mean(arriving * unit, axis=-1, keepdims=True)))
            )
        nows = [states[0, seq, :, lanes] for seq, head, lanes in chains]
        laters = [grad_state[seq, head] for seq, head, lanes in chains]
        updates = [adjusted[0, seq, :, lanes] for seq, head, lanes in chains]
        highs = [narrow(now) for now in nows]
        reads = [
            dot_nn(
                key, jnp.concatenate([high, narrow(now - high.astype(F32)), narrow(later)], axis=1)
            )
            for key, high, now, later in zip(keys, highs, nows, laters)
        ]
        scores_t = [
            narrow(jnp.where(row <= col, dot_nt(key, query), 0.0)) for key, query in zip(keys, queries)
        ]
        grams = [dot_nt(key, key) for key in keys]
        grad_updates = [
            read[:, 2 * HEAD_DIM :] + dot_nn(score, grad_out)
            for read, score, grad_out in zip(reads, scores_t, grad_outs)
        ]
        grad_targets = [
            grad_update + dot_nn(inverse[0, seq, :, lanes], grad_update)
            for grad_update, (seq, head, lanes) in zip(grad_updates, chains)
        ]
        grad_remains = [beta * grad_target for beta, grad_target in zip(betas, grad_targets)]
        rounded = [narrow(grad_remain) for grad_remain in grad_remains]
        earlier = [
            later
            + dot_tn(
                jnp.concatenate([query, key], axis=0), jnp.concatenate([grad_out, -grad_remain], axis=0)
            )
            for later, query, key, grad_out, grad_remain in zip(laters, queries, keys, grad_outs, rounded)
        ]
        for (seq, head, lanes), value in zip(chains, earlier):
            grad_state[seq, head] = value
        lowers = [
            dot_nt(jnp.concatenate([grad_out, narrow(grad_target)], axis=0), update)
            for grad_out, grad_target, update in zip(grad_outs, grad_targets, updates)
        ]
        uppers = [
            dot_nt(update, jnp.concatenate([grad_out, grad_remain], axis=0))
            for update, grad_out, grad_remain in zip(updates, grad_outs, rounded)
        ]
        by_states = [
            dot_nt(jnp.concatenate([grad_out, grad_remain], axis=0), high)
            for grad_out, grad_remain, high in zip(grad_outs, rounded, highs)
        ]
        by_laters = [dot_nt(update, later) for update, later in zip(updates, laters)]
        by_keys = []
        for index, (seq, head, lanes) in enumerate(chains):
            lower, upper, read, beta = lowers[index], uppers[index], reads[index], betas[index]
            remain = values[index].astype(F32) - (
                read[:, :HEAD_DIM] + read[:, HEAD_DIM : 2 * HEAD_DIM]
            )
            grad_lower = jnp.where(row > col, lower[CHUNK:], 0.0)
            grad_beta = jnp.sum(
                grad_targets[index] * remain - grad_lower * grams[index], axis=-1, keepdims=True
            )
            grad_logits[0, seq, :, head : head + 1] = grad_beta * beta * (1.0 - beta)
            grad_gram = -beta * grad_lower - jnp.where(row < col, upper[:, CHUNK:], 0.0)
            grad_scores = jnp.where(row >= col, lower[:CHUNK], 0.0)
            by_keys.append(
                dot_nn(
                    jnp.concatenate([narrow(grad_scores), narrow(grad_gram)], axis=0), keys[index]
                )
            )
        by_queries = [
            dot_nn(jnp.where(row <= col, upper[:, :CHUNK], 0.0), query)
            for upper, query in zip(uppers, queries)
        ]
        for index, (seq, head, lanes) in enumerate(chains):
            by_key, by_state, scale = by_keys[index], by_states[index], scales[index]
            grad_query = by_key[:CHUNK] + by_state[:CHUNK]
            grad_key = by_key[CHUNK:] - by_state[CHUNK:] + by_queries[index] + by_laters[index]
            along = jnp.sum(lengths[index] * grad_key, axis=-1, keepdims=True)
            grad_key = scale * (grad_key - lengths[index] * (scale * scale * along))
            for position, grad_act in enumerate((grad_query, grad_key, grad_remains[index])):
                trailing[seq, position, pl.ds(0, CHUNK), lanes] = grad_act * slopes[index][position]
        for seq, head, lanes in chains:
            for position in range(3):
                kept = trailing[seq, position, pl.ds(0, CHUNK), lanes]
                total = None
                for offset in range(4):
                    taps_sum[position, offset, :, lanes] += fold_rows(
                        kept * padded[seq, position, pl.ds(5 + offset, CHUNK), lanes]
                    )
                    term = taps[position, offset : offset + 1, lanes] * trailing[
                        seq, position, pl.ds(3 - offset, CHUNK), lanes
                    ]
                    total = term if total is None else total + term
                grad_projected[position, 0, seq, :, lanes] = narrow(total)

    @pl.when(step == last)
    def _():
        grad_state_out[...] = grad_state[...]
        after_out[...] = trailing[:, :, pl.ds(0, 8), :]
        grad_taps[...] = jnp.sum(taps_sum[...], axis=2)
        grad_gain[...] = jnp.sum(gain_sum[...], axis=0, keepdims=True)


def specs_for(shape, at):
    _, seqs, _, channels = shape

    def rows(width=channels):
        return pl.BlockSpec((1, seqs, CHUNK, width), lambda t, o: (o[0, at(t)], 0, o[1, at(t)], 0))

    planes = pl.BlockSpec(
        (4, 1, seqs, CHUNK, channels), lambda t, o: (0, o[0, at(t)], 0, o[1, at(t)], 0)
    )

    def whole(*shape):
        return pl.BlockSpec(shape, lambda t, o: (0,) * len(shape))

    return rows, planes, whole


def delta_forward(order, projected, logits, taps, gain, state_in, halo_in):
    shape = projected.shape[1:]
    seqs, channels = shape[1], shape[3]
    heads = channels // HEAD_DIM
    steps = shape[0] * shape[2] // CHUNK
    rows, planes, whole = specs_for(shape, lambda t: t)
    return pl.pallas_call(
        forward_kernel,
        out_shape=[
            jax.ShapeDtypeStruct(shape, dtype) for dtype in (BF16, F32, BF16, F32, BF16)
        ]
        + [jax.ShapeDtypeStruct((seqs, heads, HEAD_DIM, HEAD_DIM), F32)],
        grid_spec=pltpu.PrefetchScalarGridSpec(
            num_scalar_prefetch=1,
            grid=(steps,),
            in_specs=[
                planes,
                rows(heads),
                whole(3, 4, channels),
                whole(1, HEAD_DIM),
                whole(seqs, heads, HEAD_DIM, HEAD_DIM),
                whole(seqs, 3, 8, channels),
            ],
            out_specs=[rows() for _ in range(5)] + [whole(seqs, heads, HEAD_DIM, HEAD_DIM)],
            scratch_shapes=[
                pltpu.VMEM((seqs, heads, HEAD_DIM, HEAD_DIM), F32),
                pltpu.VMEM((seqs, 3, CHUNK + 8, channels), F32),
            ],
        ),
        compiler_params=pltpu.CompilerParams(
            dimension_semantics=("arbitrary",), vmem_limit_bytes=56 * 2**20
        ),
        cost_estimate=BRIEF,
        name="delta_forward",
    )(order, projected, logits, taps, gain, state_in, halo_in)


def delta_backward(
    order, projected, logits, taps, gain, halo_in, grad_gated, saved, grad_state_in, after_in
):
    shape = projected.shape[1:]
    seqs, channels = shape[1], shape[3]
    heads = channels // HEAD_DIM
    steps = shape[0] * shape[2] // CHUNK
    rows, planes, whole = specs_for(shape, lambda t: steps - 1 - t)
    part = CHUNK // 8

    def at_before(t, o):
        place = jnp.maximum(steps - 2 - t, 0)
        return (0, o[0, place], 0, o[1, place] * part + part - 1, 0)

    state_block = whole(seqs, heads, HEAD_DIM, HEAD_DIM)
    edge_block = whole(seqs, 3, 8, channels)
    return pl.pallas_call(
        backward_kernel,
        out_shape=[
            jax.ShapeDtypeStruct((4,) + shape, BF16),
            jax.ShapeDtypeStruct(shape[:3] + (heads,), F32),
            jax.ShapeDtypeStruct((3, 4, channels), F32),
            jax.ShapeDtypeStruct((1, HEAD_DIM), F32),
            jax.ShapeDtypeStruct((seqs, heads, HEAD_DIM, HEAD_DIM), F32),
            jax.ShapeDtypeStruct((seqs, 3, 8, channels), F32),
        ],
        grid_spec=pltpu.PrefetchScalarGridSpec(
            num_scalar_prefetch=1,
            grid=(steps,),
            in_specs=[
                planes,
                pl.BlockSpec((3, 1, seqs, 8, channels), at_before),
                rows(heads),
                whole(3, 4, channels),
                whole(1, HEAD_DIM),
                edge_block,
            ]
            + [rows() for _ in range(5)]
            + [state_block, edge_block],
            out_specs=[
                planes,
                rows(heads),
                whole(3, 4, channels),
                whole(1, HEAD_DIM),
                state_block,
                edge_block,
            ],
            scratch_shapes=[
                pltpu.VMEM((seqs, heads, HEAD_DIM, HEAD_DIM), F32),
                pltpu.VMEM((seqs, 3, CHUNK + 8, channels), F32),
                pltpu.VMEM((seqs, 3, CHUNK + 8, channels), F32),
                pltpu.VMEM((3, 4, 8, channels), F32),
                pltpu.VMEM((8, HEAD_DIM), F32),
            ],
        ),
        compiler_params=pltpu.CompilerParams(
            dimension_semantics=("arbitrary",), vmem_limit_bytes=60 * 2**20
        ),
        cost_estimate=BRIEF,
        name="delta_backward",
    )(
        order,
        projected,
        projected,
        logits,
        taps,
        gain,
        halo_in,
        grad_gated,
        *saved,
        grad_state_in,
        after_in,
    )


def weight_kernel(left_count, right_count, planes, deps, order, *refs):
    lefts, rights = refs[: 4 * left_count], refs[4 * left_count : 4 * left_count + right_count]
    outs, turned = refs[4 * left_count + right_count + deps : -1], refs[-1]
    rows, columns = lefts[0].shape

    @pl.when(pl.program_id(0) == 0)
    def _():
        for piece in range(left_count):
            for outer in range(4):
                turned[pl.ds(outer * columns, columns), pl.ds(piece * rows, rows)] = lefts[
                    4 * piece + outer
                ][...].T

    total = None
    size = turned.shape[1] // right_count
    for piece in range(right_count):
        right = rights[piece][0] if planes else rights[piece][...]
        term = lax.dot_general(
            turned[:, pl.ds(piece * size, size)],
            right,
            (((1,), (0,)), ((), ())),
            preferred_element_type=F32,
        )
        total = term if total is None else total + term
    total = narrow(total)
    for plane, out in enumerate(outs):

        @pl.when(pl.program_id(0) == plane)
        def _():
            for outer in range(4):
                out[outer] = total[outer * columns : (outer + 1) * columns]


def weight_products(order, lefts, rights, deps=()):
    rows, width = lefts[0].shape
    all_rows = rows * len(lefts)
    columns = width // 8
    planes, right_rows, size = rights[0].shape

    def pick(outer):
        return lambda n, order: (0, order[outer])

    return pl.pallas_call(
        functools.partial(weight_kernel, len(lefts), len(rights), planes, len(deps)),
        out_shape=[jax.ShapeDtypeStruct((4, columns, size), BF16)] * planes,
        grid_spec=pltpu.PrefetchScalarGridSpec(
            num_scalar_prefetch=1,
            grid=(planes,),
            in_specs=[
                pl.BlockSpec((rows, columns), pick(outer), pipeline_mode=pl.Buffered(1))
                for _ in lefts
                for outer in range(4)
            ]
            + [pl.BlockSpec((1, right_rows, size), lambda n, order: (n, 0, 0))] * len(rights)
            + [pl.BlockSpec(memory_space=pl.ANY)] * len(deps),
            out_specs=[pl.BlockSpec((4, columns, size), lambda n, order: (0, 0, 0))] * planes,
            scratch_shapes=[pltpu.VMEM((4 * columns, all_rows), BF16)],
        ),
        compiler_params=pltpu.CompilerParams(
            dimension_semantics=("arbitrary",), vmem_limit_bytes=60 * 2**20
        ),
        cost_estimate=BRIEF,
        name="weight_products",
    )(order, *[left for left in lefts for _ in range(4)], *rights, *deps)


def feed_kernel(blocks, deps, *refs):
    normed_refs, grad_refs = refs[:blocks], refs[blocks : 2 * blocks]
    w_up_hbm, w_down_hbm = refs[2 * blocks : 2 * blocks + 2]
    refs = refs[2 * blocks + 2 + deps :]
    hidden, gate_grad, out, back = refs[:4]
    w_up, w_down, normed_rows, grad_rows, row_sems, sems = refs[4:]
    step = pl.program_id(0)
    slot = step % 2
    weights = [
        pltpu.make_async_copy(w_up_hbm.at[0], w_up.at[0], sems.at[0]),
        pltpu.make_async_copy(w_up_hbm.at[1], w_up.at[1], sems.at[1]),
        pltpu.make_async_copy(w_down_hbm, w_down, sems.at[2]),
    ]

    def fetch(place, into):
        return [
            pltpu.make_async_copy(normed_refs[place], normed_rows.at[into], row_sems.at[0, into]),
            pltpu.make_async_copy(grad_refs[place], grad_rows.at[into], row_sems.at[1, into]),
        ]

    @pl.when(step == 0)
    def _():
        first = fetch(0, 0)
        first[0].start()
        weights[0].start()
        weights[1].start()
        first[1].start()
        weights[2].start()

    for here in range(1, blocks):

        @pl.when(step == here - 1)
        def _():
            for copy in fetch(here, here % 2):
                copy.start()

    arrived = fetch(0, slot)
    arrived[0].wait()

    @pl.when(step == 0)
    def _():
        weights[0].wait()

    normed = normed_rows[slot]
    gate = dot_nn(normed, w_up[0])

    @pl.when(step == 0)
    def _():
        weights[1].wait()

    up = dot_nn(normed, w_up[1])
    arrived[1].wait()

    @pl.when(step == 0)
    def _():
        weights[2].wait()

    grad_hidden = dot_nt(grad_rows[slot], w_down[...])
    sig = sigmoid(gate)
    act = gate * sig
    inner = narrow(act * up)
    gate_back = narrow(grad_hidden * up * slope(gate, sig))
    up_back = narrow(grad_hidden * act)
    hidden[...] = inner
    gate_grad[0] = gate_back
    gate_grad[1] = up_back
    out[...] = narrow(dot_nn(inner, w_down[...]))
    back[...] = narrow(dot_nt(gate_back, w_up[0]) + dot_nt(up_back, w_up[1]))


def feed_forward(normed, grads, w_up, w_down, deps=()):
    blocks = len(normed)
    rows, width = normed[0].shape
    size = w_down.shape[0]
    anywhere = pl.BlockSpec(memory_space=pl.ANY)
    wide = jax.ShapeDtypeStruct((rows * blocks, width), BF16)
    return pl.pallas_call(
        functools.partial(feed_kernel, blocks, len(deps)),
        out_shape=[
            jax.ShapeDtypeStruct((rows * blocks, size), BF16),
            jax.ShapeDtypeStruct((2, rows * blocks, size), BF16),
            wide,
            wide,
        ],
        grid=(blocks,),
        in_specs=[anywhere] * (2 * blocks + 2 + len(deps)),
        out_specs=[
            pl.BlockSpec((rows, size), lambda i: (i, 0)),
            pl.BlockSpec((2, rows, size), lambda i: (0, i, 0)),
            pl.BlockSpec((rows, width), lambda i: (i, 0)),
            pl.BlockSpec((rows, width), lambda i: (i, 0)),
        ],
        scratch_shapes=[
            pltpu.VMEM((2, width, size), BF16),
            pltpu.VMEM((size, width), BF16),
            pltpu.VMEM((2, rows, width), BF16),
            pltpu.VMEM((2, rows, width), BF16),
            pltpu.SemaphoreType.DMA((2, 2)),
            pltpu.SemaphoreType.DMA((3,)),
        ],
        compiler_params=pltpu.CompilerParams(
            dimension_semantics=("arbitrary",), vmem_limit_bytes=60 * 2**20
        ),
        cost_estimate=BRIEF,
        name="feed_forward",
    )(*normed, *grads, w_up, w_down, *deps)


def rows_kernel(blocks, planes, transposed, deps, *refs):
    row_refs, weight_hbm = refs[:blocks], refs[blocks]
    out, weight, now, row_sems, sems = refs[blocks + 1 + deps :]
    step = pl.program_id(0)
    slot = step % 2
    loads = [
        pltpu.make_async_copy(weight_hbm.at[plane], weight.at[plane], sems.at[plane])
        for plane in range(planes)
    ]

    def fetch(place, into):
        return pltpu.make_async_copy(row_refs[place], now.at[into], row_sems.at[into])

    @pl.when(step == 0)
    def _():
        fetch(0, 0).start()
        for load in loads:
            load.start()

    for here in range(1, blocks):

        @pl.when(step == here - 1)
        def _():
            fetch(here, here % 2).start()

    fetch(0, slot).wait()
    value = now[slot]
    for plane in range(planes):

        @pl.when(step == 0)
        def _():
            loads[plane].wait()

        out[plane] = (dot_nt if transposed else dot_nn)(value, weight[plane]).astype(out.dtype)


def rows_product(blocks, weight, transposed, dtype, deps=()):
    rows, width = blocks[0].shape
    planes = weight.shape[0]
    size = weight.shape[1] if transposed else weight.shape[2]
    anywhere = pl.BlockSpec(memory_space=pl.ANY)
    count = len(blocks)
    return pl.pallas_call(
        functools.partial(rows_kernel, count, planes, transposed, len(deps)),
        out_shape=jax.ShapeDtypeStruct((planes, rows * count, size), dtype),
        grid=(count,),
        in_specs=[anywhere] * (count + 1 + len(deps)),
        out_specs=pl.BlockSpec((planes, rows, size), lambda i: (0, i, 0)),
        scratch_shapes=[
            pltpu.VMEM(weight.shape, BF16),
            pltpu.VMEM((2, rows, width), BF16),
            pltpu.SemaphoreType.DMA((2,)),
            pltpu.SemaphoreType.DMA((planes,)),
        ],
        compiler_params=pltpu.CompilerParams(
            dimension_semantics=("arbitrary",), vmem_limit_bytes=60 * 2**20
        ),
        cost_estimate=BRIEF,
        name="rows_product",
    )(*blocks, weight, *deps)


def input_kernel(planes, deps, *refs):
    grad, logit, weight_hbm, beta_weight = refs[:4]
    away, near, weight, sems = refs[4 + deps :]
    step = pl.program_id(0)
    loads = [
        pltpu.make_async_copy(weight_hbm.at[plane], weight.at[plane], sems.at[plane])
        for plane in range(planes)
    ]

    @pl.when(step == 0)
    def _():
        for load in loads:
            load.start()

    total = dot_nt(logit[...], beta_weight[...])
    for plane in range(planes):

        @pl.when(step == 0)
        def _():
            loads[plane].wait()

        total = total + dot_nt(grad[plane], weight[plane])
    total = narrow(total)
    half = pl.num_programs(0) // 2

    @pl.when(step < half)
    def _():
        away[...] = total

    @pl.when(step >= half)
    def _():
        near[...] = total


def input_product(grad, logit, weight, beta_weight, block, deps=()):
    planes, rows, size = grad.shape
    width = weight.shape[1]
    count = rows // block
    half = count // 2
    place = lambda i: (i + half) % count
    anywhere = pl.BlockSpec(memory_space=pl.ANY)
    return pl.pallas_call(
        functools.partial(input_kernel, planes, len(deps)),
        out_shape=[jax.ShapeDtypeStruct((rows // 2, width), BF16)] * 2,
        grid=(count,),
        in_specs=[
            pl.BlockSpec((planes, block, size), lambda i: (0, place(i), 0)),
            pl.BlockSpec((block, logit.shape[1]), lambda i: (place(i), 0)),
            anywhere,
            pl.BlockSpec(beta_weight.shape, lambda i: (0, 0)),
        ]
        + [anywhere] * len(deps),
        out_specs=[
            pl.BlockSpec((block, width), lambda i: (jnp.minimum(i, half - 1), 0)),
            pl.BlockSpec((block, width), lambda i: (jnp.maximum(i - half, 0), 0)),
        ],
        scratch_shapes=[pltpu.VMEM(weight.shape, BF16), pltpu.SemaphoreType.DMA((planes,))],
        compiler_params=pltpu.CompilerParams(
            dimension_semantics=("arbitrary",), vmem_limit_bytes=60 * 2**20
        ),
        cost_estimate=BRIEF,
        name="input_product",
    )(grad, logit, weight, beta_weight, *deps)


def rms_scale(signal, gain):
    return signal * lax.rsqrt(jnp.mean(signal * signal, axis=-1, keepdims=True) + EPS) * gain


def rms_back(signal, gain, grad):
    rate = lax.rsqrt(jnp.mean(signal * signal, axis=-1, keepdims=True) + EPS)
    unit = signal * rate
    scaled = grad * gain
    grad_signal = rate * (scaled - unit * jnp.mean(scaled * unit, axis=-1, keepdims=True))
    return grad_signal, jnp.sum(grad * unit, axis=0)


def tie(*values):
    return lax.optimization_barrier(values)


def hold(value, *others):
    return tie(value, *others)[0]


def swap(value, axis, distance):
    size = lax.axis_size(axis)
    return lax.ppermute(value, axis, [(place, place ^ distance) for place in range(size)])


def sum_over(value, axis):
    distance = 1
    while distance < lax.axis_size(axis):
        value = value + swap(value, axis, distance)
        distance *= 2
    return value


def own_scale(group_ids, group_weight, seqs_here, own_seq):
    group_range = jnp.arange(GROUPS, dtype=jnp.int32)
    member = (group_ids[:, None] == group_range[None, :]).astype(jnp.int32)
    counts = sum_over(jnp.sum(member, axis=0) * LEN, "dp").astype(F32)
    member_float = member.astype(F32)
    seq_weight = jnp.sum(member_float * group_weight.astype(F32)[None, :], axis=1)
    seq_count = jnp.sum(member_float * counts[None, :], axis=1)
    total_tokens = LEN * seqs_here * lax.axis_size("dp")
    seq_scale = seq_weight * total_tokens / (GROUPS * seq_count)
    return jnp.sum(jnp.where(jnp.arange(seqs_here) == own_seq, seq_scale, 0.0))


def sum_small(grad_beta, grad_taps, gain_one, gain_two, gain_heads):
    beta_size, taps_size, width = grad_beta.size, grad_taps.size, gain_one.size
    small = sum_over(
        jnp.concatenate(
            [grad_beta.reshape(-1), grad_taps.reshape(-1), gain_one, gain_two, gain_heads]
        ),
        "dp",
    )
    gains = sum_over(small[beta_size + taps_size :], "head")
    return (
        small[:beta_size].reshape(grad_beta.shape),
        small[beta_size : beta_size + taps_size].reshape(grad_taps.shape),
        gains[:width],
        gains[width : 2 * width],
        gains[2 * width :],
    )


def plain_body(
    tokens,
    norm_gain,
    w_proj,
    w_beta,
    conv_weight,
    head_gain,
    w_out,
    ffn_gain,
    w_ffn,
    w_down,
    group_ids,
    group_weight,
    cotangent,
):
    rows_here = tokens.shape[0]
    head_pos = lax.axis_index("head")
    seqs = rows_here * lax.axis_size("head") // LEN
    channels = w_proj.shape[2]
    heads = channels // HEAD_DIM
    gain_one, gain_two = norm_gain.astype(F32), ffn_gain.astype(F32)
    gain_heads, taps = head_gain.astype(F32)[None], conv_weight.astype(F32)

    def gather(rows):
        return lax.all_gather(narrow(rows), "head", axis=0, tiled=True)

    def scatter(partial):
        return lax.psum_scatter(narrow(partial), "head", scatter_dimension=0, tiled=True).astype(F32)

    def scatter_weight(product, dim):
        return lax.psum_scatter(narrow(product), "dp", scatter_dimension=dim, tiled=True).astype(F32)

    def product(form, left, right):
        return jnp.einsum(form, left, right, preferred_element_type=F32)

    x_here = tokens.astype(F32)
    scale = own_scale(group_ids, group_weight, seqs, (head_pos * rows_here) // LEN)
    upstream = cotangent.astype(F32) * scale
    normed = gather(rms_scale(x_here, gain_one))
    grad_ffn = gather(upstream)
    steps = LEN // CHUNK
    order = jnp.stack([jnp.zeros(steps, jnp.int32), jnp.arange(steps, dtype=jnp.int32)])

    def by_seq(rows):
        return rows.reshape(rows.shape[:-2] + (1, seqs, LEN, rows.shape[-1]))

    def flat(rows):
        return rows.reshape(rows.shape[:-4] + (seqs * LEN, rows.shape[-1]))

    projected = by_seq(product("td,fdk->ftk", normed, w_proj))
    logits = by_seq(product("td,dh->th", normed, w_beta))
    state = jnp.zeros((seqs, heads, HEAD_DIM, HEAD_DIM), F32)
    halo = jnp.zeros((seqs, 3, 8, channels), F32)
    gated, *saved, _ = delta_forward(order, projected, logits, taps, gain_heads, state, halo)
    gated = flat(gated)
    middle = x_here + scatter(product("tk,kd->td", gated, w_out))
    normed_two = gather(rms_scale(middle, gain_two))
    gate_up = product("td,fdk->ftk", normed_two, w_ffn)
    grad_hidden = product("td,fd->tf", grad_ffn, w_down)
    sig = sigmoid(gate_up[0])
    act = gate_up[0] * sig
    hidden = narrow(act * gate_up[1])
    gate_grad = jnp.stack(
        [narrow(grad_hidden * gate_up[1] * slope(gate_up[0], sig)), narrow(grad_hidden * act)]
    )
    mixed_out = narrow(middle + scatter(product("tk,kd->td", hidden, w_down)))
    through, gain_two_sum = rms_back(
        middle, gain_two, scatter(product("ftk,fdk->td", gate_grad, w_ffn))
    )
    grad_middle = upstream + through
    grad_mixer = gather(grad_middle)
    back, logit_back, taps_back, gain_back, _, _ = delta_backward(
        order,
        projected,
        logits,
        taps,
        gain_heads,
        halo,
        by_seq(product("td,kd->tk", grad_mixer, w_out)),
        saved,
        state,
        halo,
    )
    back, logit_back = flat(back), narrow(flat(logit_back))
    grad_normed = scatter(
        product("ftk,fdk->td", back, w_proj) + product("th,dh->td", logit_back, w_beta)
    )
    through, gain_one_sum = rms_back(x_here, gain_one, grad_normed)
    beta, conv, gain_one_sum, gain_two_sum, gain_back = sum_small(
        product("td,th->dh", normed, logit_back), taps_back, gain_one_sum, gain_two_sum, gain_back[0]
    )
    return (
        mixed_out,
        grad_middle + through,
        gain_one_sum,
        scatter_weight(product("td,ftk->fdk", normed, back), 1),
        beta,
        conv,
        gain_back,
        scatter_weight(product("tk,td->kd", gated, grad_mixer), 1),
        gain_two_sum,
        scatter_weight(product("td,ftk->fdk", normed_two, gate_grad), 1),
        scatter_weight(product("tf,td->fd", hidden, grad_ffn), 1),
    )


def pair_sum(away, near):
    return near.astype(F32) + swap(away, "head", 1).astype(F32)


def own_half(total):
    return total[: total.shape[0] // 2]


def far_half(total):
    return swap(narrow(total[total.shape[0] // 2 :]), "head", 2)


def paired_body(
    tokens,
    norm_gain,
    w_proj,
    w_beta,
    conv_weight,
    head_gain,
    w_out,
    ffn_gain,
    w_ffn,
    w_down,
    group_ids,
    group_weight,
    cotangent,
):
    rows_here, width = tokens.shape
    head_pos = lax.axis_index("head")
    core = head_pos % 2
    place = lax.axis_index("dp")
    outer, inner = place // 2, place % 2
    seqs = 2
    channels = w_proj.shape[2]
    heads = channels // HEAD_DIM
    half = rows_here // 2
    gain_one, gain_two = norm_gain.astype(F32), ffn_gain.astype(F32)
    gain_heads, taps = head_gain.astype(F32)[None], conv_weight.astype(F32)

    def deal(rows):
        first, second = rows[:half], rows[half:]
        other = swap(jnp.where(core == 0, second, first), "head", 1)
        return jnp.where(core == 0, first, other), jnp.where(core == 0, other, second)

    def undeal(early, late):
        other = swap(jnp.where(core == 0, late, early), "head", 1)
        return jnp.concatenate(
            [jnp.where(core == 0, early, other), jnp.where(core == 0, other, late)], axis=0
        )

    def product(left, right):
        return jnp.dot(left, right, preferred_element_type=F32)

    split = half // CHUNK
    step_range = jnp.arange(2 * split, dtype=jnp.int32)
    order = jnp.stack([(step_range // split) ^ core, step_range % split])

    def by_seq(rows):
        return rows.reshape(rows.shape[:-2] + (2, seqs, half, rows.shape[-1]))

    def flat(rows):
        return rows.reshape(rows.shape[:-4] + (2 * seqs * half, rows.shape[-1]))

    near_order = 2 * (outer ^ jnp.array([0, 2, 1, 3], dtype=jnp.int32)) + inner
    away_order = near_order ^ 1

    def far_of(rows):
        return swap(rows, "head", 2)

    def blocks(rows, far):
        return [rows, far, swap(rows, "head", 1), swap(far, "head", 1)]

    def logits_of(normed):
        return jnp.concatenate([product(block, w_beta) for block in normed], axis=0)

    def mixer_out(gated):
        count = gated.shape[0] // 2
        return pair_sum(narrow(product(gated[count:], w_out)), product(gated[:count], w_out))

    def send(products):
        return [swap(value, "dp", 1) for value in products]

    def halve(kept, away):
        return swap(narrow(kept[2:].astype(F32) + away[2:].astype(F32)), "dp", 2)

    def halve_again(kept, away, first):
        return swap(
            narrow(kept[1].astype(F32) + away[1].astype(F32) + first[1].astype(F32)), "dp", 4
        )

    def finish(kept, away, first, second):
        return (
            kept[0].astype(F32) + away[0].astype(F32) + first[0].astype(F32) + second.astype(F32)
        )

    x_a, x_b = [part.astype(F32) for part in deal(tokens)]
    rows_a, rows_b = narrow(rms_scale(x_a, gain_one)), narrow(rms_scale(x_b, gain_one))
    far_a = far_of(rows_a)
    normed_a = blocks(rows_a, far_a)
    scale = own_scale(group_ids, group_weight, seqs, head_pos // 2)
    up_a, up_b = [part.astype(F32) * scale for part in deal(cotangent)]
    up_rows_a, up_rows_b = narrow(up_a), narrow(up_b)
    far_b = far_of(rows_b)
    up_far_a = far_of(hold(up_rows_a, far_a))

    state = jnp.zeros((seqs, heads, HEAD_DIM, HEAD_DIM), F32)
    halo_a = jnp.zeros((seqs, 3, 8, channels), F32)
    projected_a = by_seq(rows_product(normed_a, w_proj, False, F32))
    logits_a = by_seq(logits_of(normed_a))
    gated_a, *saved_a, state_a = delta_forward(
        order, projected_a, logits_a, taps, gain_heads, state, halo_a
    )
    gated_a = flat(gated_a)
    halo_b = lax.dynamic_slice(
        projected_a, (0, 1 - core, 0, half - 8, 0), (3, 1, seqs, 8, channels)
    )[:, 0].transpose(1, 0, 2, 3)
    gated_a, far_b, up_far_a = lax.optimization_barrier((gated_a, far_b, up_far_a))
    mixer_a = mixer_out(gated_a)
    mixer_far_a = far_half(mixer_a)
    up_far_b = far_of(hold(up_rows_b, mixer_a))

    normed_b = blocks(rows_b, far_b)
    grad_ffn_a = blocks(up_rows_a, up_far_a)
    projected_b = by_seq(rows_product(hold(normed_b, mixer_a), w_proj, False, F32))
    logits_b = by_seq(logits_of(normed_b))
    gated_b, *saved_b, _ = delta_forward(
        order, projected_b, logits_b, taps, gain_heads, state_a, halo_b
    )
    gated_b = flat(gated_b)
    gated_b, mixer_far_a, up_far_b = lax.optimization_barrier((gated_b, mixer_far_a, up_far_b))
    middle_a = x_a + own_half(mixer_a) + mixer_far_a.astype(F32)
    rows_a = narrow(rms_scale(middle_a, gain_two))
    two_far_a = far_of(rows_a)
    mixer_b = mixer_out(hold(gated_b, rows_a))
    mixer_far_b = far_half(mixer_b)
    two_a = blocks(rows_a, hold(two_far_a, mixer_b))
    grad_ffn_b = blocks(up_rows_b, up_far_b)

    def feed(normed, grads):
        return feed_forward(normed, grads, w_ffn, w_down)

    away_a = feed(two_a[2:], grad_ffn_a[2:])
    away_a, mixer_far_b = lax.optimization_barrier((away_a, mixer_far_b))
    middle_b = x_b + own_half(mixer_b) + mixer_far_b.astype(F32)
    rows_b = narrow(rms_scale(middle_b, gain_two))
    two_far_b = far_of(rows_b)
    near_a = feed(hold(two_a[:2], rows_b), grad_ffn_a[:2])
    near_a, two_far_b = lax.optimization_barrier((near_a, two_far_b))
    back_a = pair_sum(away_a[3], near_a[3])
    back_far_a = far_half(back_a)
    out_a = pair_sum(away_a[2], hold(near_a[2], back_a))
    out_far_a = far_half(out_a)
    two_b = blocks(rows_b, two_far_b)
    away_b = feed(hold(two_b[2:], back_a, out_a), grad_ffn_b[2:])
    away_b, back_far_a = lax.optimization_barrier((away_b, back_far_a))
    through, gain_two_a = rms_back(middle_a, gain_two, own_half(back_a) + back_far_a.astype(F32))
    grad_middle_a = up_a + through
    mix_rows_a = narrow(grad_middle_a)
    mix_far_a = far_of(mix_rows_a)
    near_b = feed(hold(two_b[:2], mix_rows_a), grad_ffn_b[:2])
    near_b, mix_far_a, out_far_a = lax.optimization_barrier((near_b, mix_far_a, out_far_a))
    back_b = pair_sum(away_b[3], near_b[3])
    back_far_b = far_half(back_b)

    down_left = grad_ffn_a + grad_ffn_b
    down_right = [part[0][None] for part in (near_a, away_a, near_b, away_b)]
    up_left = two_a + two_b
    up_right = [part[1] for part in (near_a, away_a, near_b, away_b)]
    down_sent = weight_products(hold(away_order, back_b), down_left, down_right)
    (down_away,) = send(down_sent)
    up_sent = weight_products(hold(away_order, *down_sent), up_left, up_right)
    up_sent, back_far_b = lax.optimization_barrier((up_sent, back_far_b))
    up_away_0, up_away_1 = send(up_sent)
    through, gain_two_b = rms_back(middle_b, gain_two, own_half(back_b) + back_far_b.astype(F32))
    grad_middle_b = up_b + through
    mix_rows_b = narrow(grad_middle_b)
    mix_far_b = far_of(mix_rows_b)
    out_b = pair_sum(away_b[2], hold(near_b[2], mix_rows_b))
    out_far_b = far_half(out_b)
    (down_kept,) = weight_products(hold(near_order, mix_rows_b, out_b), down_left, down_right)
    w_out_plane = w_out[None]
    grad_mixer_a = blocks(mix_rows_a, mix_far_a)
    grad_gated_a = rows_product(hold(grad_mixer_a, down_kept), w_out_plane, True, F32)[0]
    grad_gated_a, mix_far_b = lax.optimization_barrier((grad_gated_a, mix_far_b))
    grad_mixer_b = blocks(mix_rows_b, mix_far_b)
    grad_gated_b = rows_product(hold(grad_mixer_b, grad_gated_a), w_out_plane, True, F32)[0]
    grad_gated_b, down_away = lax.optimization_barrier((grad_gated_b, down_away))
    down_first = halve(down_kept, down_away)

    zero_state = jnp.zeros((seqs, heads, HEAD_DIM, HEAD_DIM), F32)
    zero_after = jnp.zeros((seqs, 3, 8, channels), F32)
    late = delta_backward(
        order,
        projected_b,
        logits_b,
        taps,
        gain_heads,
        halo_b,
        by_seq(grad_gated_b),
        saved_b,
        zero_state,
        zero_after,
    )
    late, down_first, out_far_b = tie(late, down_first, out_far_b)
    proj_b, logit_b, taps_b, gain_heads_b, grad_state, after = late
    down_second = halve_again(down_kept, down_away, down_first)
    up_kept_0, up_kept_1 = weight_products(hold(near_order, grad_state), up_left, up_right)
    up_kept_0, up_kept_1, up_away_0 = lax.optimization_barrier((up_kept_0, up_kept_1, up_away_0))
    up_first_0 = halve(up_kept_0, up_away_0)
    out_left, out_right = grad_mixer_a + grad_mixer_b, [gated_a[None], gated_b[None]]
    (out_sent,) = weight_products(hold(away_order, up_kept_0), out_left, out_right)
    (out_away,) = send([out_sent])
    early = delta_backward(
        order,
        projected_a,
        logits_a,
        taps,
        gain_heads,
        halo_a,
        by_seq(grad_gated_a),
        saved_a,
        hold(grad_state, out_sent),
        after,
    )
    early, up_first_0, down_second = lax.optimization_barrier((early, up_first_0, down_second))
    proj_a, logit_a, taps_a, gain_heads_a, _, _ = early
    proj_a, proj_b = flat(proj_a), flat(proj_b)
    logit_a, logit_b = narrow(flat(logit_a)), narrow(flat(logit_b))
    up_second_0 = halve_again(up_kept_0, up_away_0, up_first_0)
    proj_left, proj_right = normed_a + normed_b, [proj_a, proj_b]
    proj_sent = weight_products(away_order, proj_left, proj_right)
    proj_sent, up_away_1, proj_a = tie(proj_sent, up_away_1, proj_a)
    proj_away = send(proj_sent)
    up_first_1 = halve(up_kept_1, up_away_1)
    inputs_a = input_product(proj_a, logit_a, w_proj, w_beta, half)
    inputs_a, out_away, proj_b = tie(inputs_a, out_away, proj_b)
    inputs_b = input_product(proj_b, logit_b, w_proj, w_beta, half)
    inputs_a, inputs_b, proj_away[0], proj_away[1], up_first_1 = tie(
        inputs_a, inputs_b, proj_away[0], proj_away[1], up_first_1
    )
    in_a = pair_sum(*inputs_a)
    in_b = pair_sum(*inputs_b)
    up_quarter_1 = narrow(
        up_kept_1[1].astype(F32) + up_away_1[1].astype(F32) + up_first_1[1].astype(F32)
    )
    in_a, in_b, near_order, up_quarter_1 = tie(in_a, in_b, near_order, up_quarter_1)
    up_second_1 = swap(up_quarter_1, "dp", 4)
    in_far_a = far_half(in_a)
    in_far_b = far_half(in_b)
    proj_kept = weight_products(near_order, proj_left, proj_right)
    proj_kept, proj_away[2], near_order = tie(proj_kept, proj_away[2], near_order)
    proj_first = [halve(kept, away) for kept, away in zip(proj_kept[:2], proj_away[:2])]
    (out_kept,) = weight_products(near_order, out_left, out_right)
    out_kept, proj_away[3], out_a, out_b = tie(out_kept, proj_away[3], out_a, out_b)
    proj_first += [halve(kept, away) for kept, away in zip(proj_kept[2:], proj_away[2:])]
    out_first = halve(out_kept, out_away)
    proj_second = [
        halve_again(kept, away, first)
        for kept, away, first in zip(proj_kept, proj_away, proj_first)
    ]
    out_second = halve_again(out_kept, out_away, out_first)

    mixed_out = undeal(
        narrow(middle_a + own_half(out_a) + out_far_a.astype(F32)),
        narrow(middle_b + own_half(out_b) + out_far_b.astype(F32)),
    )
    through_b, gain_one_b = rms_back(x_b, gain_one, own_half(in_b) + in_far_b.astype(F32))
    through_a, gain_one_a = rms_back(x_a, gain_one, own_half(in_a) + in_far_a.astype(F32))
    grad_tokens = undeal(grad_middle_a + through_a, grad_middle_b + through_b)
    grad_beta = 0.0
    for normed, logit in ((normed_a, logit_a), (normed_b, logit_b)):
        for index, block in enumerate(normed):
            grad_beta = grad_beta + jnp.einsum(
                "td,th->dh",
                block,
                logit[index * half : (index + 1) * half],
                preferred_element_type=F32,
            )
    beta, conv, gain_one_sum, gain_two_sum, gain_heads_sum = sum_small(
        grad_beta,
        taps_a + taps_b,
        gain_one_a + gain_one_b,
        gain_two_a + gain_two_b,
        (gain_heads_a + gain_heads_b)[0],
    )
    return (
        mixed_out,
        grad_tokens,
        gain_one_sum,
        jnp.stack(
            [finish(*parts) for parts in zip(proj_kept, proj_away, proj_first, proj_second)]
        ),
        beta,
        conv,
        gain_heads_sum,
        finish(out_kept, out_away, out_first, out_second).T,
        gain_two_sum,
        jnp.stack(
            [
                finish(up_kept_0, up_away_0, up_first_0, up_second_0),
                finish(up_kept_1, up_away_1, up_first_1, up_second_1),
            ]
        ),
        finish(down_kept, down_away, down_first, down_second).T,
    )


def body(*args):
    rows_here, channels = args[0].shape[0], args[2].shape[2]
    paired = (
        lax.axis_size("head") == 4
        and lax.axis_size("dp") == 8
        and rows_here * 2 == LEN
        and channels % HEAD_DIM == 0
    )
    return (paired_body if paired else plain_body)(*args)


def solution(mesh):
    placed = (
        P(("dp", "head"), None),
        P(),
        P(None, None, "head"),
        P(None, "head"),
        P(None, None, "head"),
        P(),
        P("head", None),
        P(),
        P(None, None, "head"),
        P("head", None),
        P("dp"),
        P(),
        P(("dp", "head"), None),
    )
    return jax.shard_map(
        body,
        mesh=mesh,
        in_specs=placed,
        out_specs=(
            P(("dp", "head"), None),
            P(("dp", "head"), None),
            P(),
            P(None, "dp", "head"),
            P(None, "head"),
            P(None, None, "head"),
            P(),
            P("head", "dp"),
            P(),
            P(None, "dp", "head"),
            P("head", "dp"),
        ),
        check_vma=False,
    )
```

```python
import functools

import jax
import jax.numpy as jnp
from jax import lax
from jax.experimental import pallas as pl
from jax.experimental.pallas import tpu as pltpu
from jax.sharding import PartitionSpec as P

HEAD_DIM = 128
CHUNK = 128
LEN = 1024
BACK_CHAINS = 4
GROUPS = 4
EPS = 1e-06
F32 = jnp.float32
BF16 = jnp.bfloat16
BRIEF = pl.CostEstimate(flops=10**9, bytes_accessed=10**6, transcendentals=0)


def narrow(value):
    return value.astype(BF16)


def dot_nn(left, right):
    return lax.dot_general(
        narrow(left), narrow(right), (((1,), (0,)), ((), ())), preferred_element_type=F32
    )


def dot_nt(left, right):
    return lax.dot_general(
        narrow(left), narrow(right), (((1,), (1,)), ((), ())), preferred_element_type=F32
    )


def dot_tn(left, right):
    return lax.dot_general(
        narrow(left), narrow(right), (((0,), (0,)), ((), ())), preferred_element_type=F32
    )


def sigmoid(value):
    return 1.0 / (1.0 + jnp.exp(-value))


def invert_lower(matrices, row, col):
    joined = row ^ col
    extras = [-jnp.where(joined == 1, below, 0.0) for below in matrices]
    size = 2
    while size < CHUNK:
        inside = (joined >= size) & (joined < 2 * size)
        corners = [jnp.where(inside, below, 0.0) for below in matrices]
        lefts = [corner + dot_nn(extra, corner) for extra, corner in zip(extras, corners)]
        extras = [extra - left - dot_nn(left, extra) for extra, left in zip(extras, lefts)]
        size *= 2
    rounded = [narrow(extra) for extra in extras]
    highs = [narrow(below) for below in matrices]
    lows = [narrow(below - high.astype(F32)) for below, high in zip(matrices, highs)]
    products = [
        dot_nn(jnp.concatenate([high, low], axis=1), jnp.concatenate([kept, kept], axis=0))
        for high, low, kept in zip(highs, lows, rounded)
    ]
    wides = [kept.astype(F32) for kept in rounded]
    residuals = [
        -(below + wide + product) for below, wide, product in zip(matrices, wides, products)
    ]
    return [
        wide + residual + dot_nn(kept, residual)
        for wide, residual, kept in zip(wides, residuals, rounded)
    ]


def activate_taps(padded, taps, position, seq, lanes):
    summed = None
    for offset in range(4):
        term = taps[position, offset : offset + 1, lanes] * padded[seq, position, pl.ds(5 + offset, CHUNK), lanes]
        summed = term if summed is None else summed + term
    return summed


def chains_of(seqs, heads):
    return [(seq, head, pl.ds(head * HEAD_DIM, HEAD_DIM)) for seq in range(seqs) for head in range(heads)]


def masks():
    row = lax.broadcasted_iota(jnp.int32, (CHUNK, CHUNK), 0)
    col = lax.broadcasted_iota(jnp.int32, (CHUNK, CHUNK), 1)
    return row, col


def forward_kernel(
    order,
    projected,
    logits,
    taps,
    gain,
    state_in,
    halo_in,
    gated,
    raw,
    inverse,
    states,
    adjusted,
    state_out,
    state,
    padded,
):
    step = pl.program_id(0)
    seqs, heads = state.shape[:2]
    chains = chains_of(seqs, heads)

    @pl.when(step == 0)
    def _():
        state[...] = state_in[...]
        padded[:, :, pl.ds(0, 8), :] = halo_in[...]

    @pl.when(step > 0)
    def _():
        padded[:, :, pl.ds(0, 8), :] = padded[:, :, pl.ds(CHUNK, 8), :]

    for seq in range(seqs):
        for position in range(3):
            padded[seq, position, pl.ds(8, CHUNK), :] = projected[position, 0, seq].astype(F32)
    row, col = masks()
    queries, keys, values, betas = [], [], [], []
    for seq, head, lanes in chains:
        acts = []
        for position in range(3):
            summed = activate_taps(padded, taps, position, seq, lanes)
            acts.append(summed * sigmoid(summed))
        scale = lax.rsqrt(jnp.sum(acts[1] * acts[1], axis=-1, keepdims=True) + EPS)
        queries.append(narrow(acts[0]))
        keys.append(narrow(acts[1] * scale))
        values.append(narrow(acts[2]))
        betas.append(sigmoid(logits[0, seq, :, head : head + 1]))
    belows = [jnp.where(row > col, beta * dot_nt(key, key), 0.0) for key, beta in zip(keys, betas)]
    scores = [
        narrow(jnp.where(row >= col, dot_nt(query, key), 0.0)) for query, key in zip(queries, keys)
    ]
    extras = [narrow(extra) for extra in invert_lower(belows, row, col)]
    nows = [state[seq, head] for seq, head, _ in chains]
    reads = []
    for query, key, now in zip(queries, keys, nows):
        high = narrow(now)
        low = narrow(now - high.astype(F32))
        read = dot_nn(jnp.concatenate([key, query], axis=0), jnp.concatenate([high, low], axis=1))
        reads.append(read[:, :HEAD_DIM] + read[:, HEAD_DIM:])
    targets = [
        beta * (value.astype(F32) - read[:CHUNK]) for beta, value, read in zip(betas, values, reads)
    ]
    updates = [narrow(target + dot_nn(extra, target)) for extra, target in zip(extras, targets)]
    outs = [
        read[CHUNK:] + dot_nn(score, update) for read, score, update in zip(reads, scores, updates)
    ]
    laters = [now + dot_tn(key, update) for now, key, update in zip(nows, keys, updates)]
    for index, (seq, head, lanes) in enumerate(chains):
        state[seq, head] = laters[index]
        raw[0, seq, :, lanes] = outs[index]
        inverse[0, seq, :, lanes] = extras[index].T
        states[0, seq, :, lanes] = nows[index]
        adjusted[0, seq, :, lanes] = updates[index]
        gate = projected[3, 0, seq, :, lanes].astype(F32)
        rate = lax.rsqrt(jnp.mean(outs[index] * outs[index], axis=-1, keepdims=True) + EPS)
        gated[0, seq, :, lanes] = narrow(outs[index] * rate * gain[...] * (gate * sigmoid(gate)))

    @pl.when(step == pl.num_programs(0) - 1)
    def _():
        state_out[...] = state[...]


def slope(value, sig):
    return sig * (1.0 + value * (1.0 - sig))


def fold_rows(value):
    return jnp.sum(value.reshape(CHUNK // 8, 8, value.shape[-1]), axis=0)


def backward_kernel(
    order,
    projected,
    before,
    logits,
    taps,
    gain,
    halo_in,
    grad_gated,
    raw,
    inverse,
    states,
    adjusted,
    grad_state_in,
    after_in,
    grad_projected,
    grad_logits,
    grad_taps,
    grad_gain,
    grad_state_out,
    after_out,
    grad_state,
    padded,
    trailing,
    taps_sum,
    gain_sum,
):
    step = pl.program_id(0)
    last = pl.num_programs(0) - 1
    seqs, heads = grad_state.shape[:2]

    @pl.when(step == 0)
    def _():
        taps_sum[...] = jnp.zeros_like(taps_sum)
        gain_sum[...] = jnp.zeros_like(gain_sum)
        grad_state[...] = grad_state_in[...]
        trailing[:, :, pl.ds(CHUNK, 8), :] = after_in[...]

    @pl.when(step > 0)
    def _():
        trailing[:, :, pl.ds(CHUNK, 8), :] = trailing[:, :, pl.ds(0, 8), :]

    @pl.when(step == last)
    def _():
        padded[:, :, pl.ds(0, 8), :] = halo_in[...]

    @pl.when(step < last)
    def _():
        for seq in range(seqs):
            for position in range(3):
                padded[seq, position, pl.ds(0, 8), :] = before[position, 0, seq].astype(F32)

    for seq in range(seqs):
        for position in range(3):
            padded[seq, position, pl.ds(8, CHUNK), :] = projected[position, 0, seq].astype(F32)
    row, col = masks()
    everything = chains_of(seqs, heads)
    for begin in range(0, len(everything), BACK_CHAINS):
        chains = everything[begin : begin + BACK_CHAINS]
        slopes, lengths, scales, queries, keys, values, betas = [], [], [], [], [], [], []
        for seq, head, lanes in chains:
            sums = [activate_taps(padded, taps, position, seq, lanes) for position in range(3)]
            sigs = [sigmoid(summed) for summed in sums]
            acts = [summed * sig for summed, sig in zip(sums, sigs)]
            slopes.append([slope(summed, sig) for summed, sig in zip(sums, sigs)])
            scale = lax.rsqrt(jnp.sum(acts[1] * acts[1], axis=-1, keepdims=True) + EPS)
            lengths.append(acts[1])
            scales.append(scale)
            queries.append(narrow(acts[0]))
            keys.append(narrow(acts[1] * scale))
            values.append(narrow(acts[2]))
            betas.append(sigmoid(logits[0, seq, :, head : head + 1]))
        grad_outs = []
        for seq, head, lanes in chains:
            out = raw[0, seq, :, lanes]
            rate = lax.rsqrt(jnp.mean(out * out, axis=-1, keepdims=True) + EPS)
            unit = out * rate
            gate = projected[3, 0, seq, :, lanes].astype(F32)
            gate_sig = sigmoid(gate)
            gate_act = gate * gate_sig
            arriving = grad_gated[0, seq, :, lanes].astype(F32)
            gain_sum[...] += fold_rows(arriving * unit * gate_act)
            arriving = arriving * gain[...]
            grad_projected[3, 0, seq, :, lanes] = narrow(arriving * unit * slope(gate, gate_sig))
            arriving = arriving * gate_act
            grad_outs.append(
                narrow(rate * (arriving - unit * jnp.mean(arriving * unit, axis=-1, keepdims=True)))
            )
        nows = [states[0, seq, :, lanes] for seq, head, lanes in chains]
        laters = [grad_state[seq, head] for seq, head, lanes in chains]
        updates = [adjusted[0, seq, :, lanes] for seq, head, lanes in chains]
        highs = [narrow(now) for now in nows]
        reads = [
            dot_nn(
                key, jnp.concatenate([high, narrow(now - high.astype(F32)), narrow(later)], axis=1)
            )
            for key, high, now, later in zip(keys, highs, nows, laters)
        ]
        scores_t = [
            narrow(jnp.where(row <= col, dot_nt(key, query), 0.0)) for key, query in zip(keys, queries)
        ]
        grams = [dot_nt(key, key) for key in keys]
        grad_updates = [
            read[:, 2 * HEAD_DIM :] + dot_nn(score, grad_out)
            for read, score, grad_out in zip(reads, scores_t, grad_outs)
        ]
        grad_targets = [
            grad_update + dot_nn(inverse[0, seq, :, lanes], grad_update)
            for grad_update, (seq, head, lanes) in zip(grad_updates, chains)
        ]
        grad_remains = [beta * grad_target for beta, grad_target in zip(betas, grad_targets)]
        rounded = [narrow(grad_remain) for grad_remain in grad_remains]
        earlier = [
            later
            + dot_tn(
                jnp.concatenate([query, key], axis=0), jnp.concatenate([grad_out, -grad_remain], axis=0)
            )
            for later, query, key, grad_out, grad_remain in zip(laters, queries, keys, grad_outs, rounded)
        ]
        for (seq, head, lanes), value in zip(chains, earlier):
            grad_state[seq, head] = value
        lowers = [
            dot_nt(jnp.concatenate([grad_out, narrow(grad_target)], axis=0), update)
            for grad_out, grad_target, update in zip(grad_outs, grad_targets, updates)
        ]
        uppers = [
            dot_nt(update, jnp.concatenate([grad_out, grad_remain], axis=0))
            for update, grad_out, grad_remain in zip(updates, grad_outs, rounded)
        ]
        by_states = [
            dot_nt(jnp.concatenate([grad_out, grad_remain], axis=0), high)
            for grad_out, grad_remain, high in zip(grad_outs, rounded, highs)
        ]
        by_laters = [dot_nt(update, later) for update, later in zip(updates, laters)]
        by_keys = []
        for index, (seq, head, lanes) in enumerate(chains):
            lower, upper, read, beta = lowers[index], uppers[index], reads[index], betas[index]
            remain = values[index].astype(F32) - (
                read[:, :HEAD_DIM] + read[:, HEAD_DIM : 2 * HEAD_DIM]
            )
            grad_lower = jnp.where(row > col, lower[CHUNK:], 0.0)
            grad_beta = jnp.sum(
                grad_targets[index] * remain - grad_lower * grams[index], axis=-1, keepdims=True
            )
            grad_logits[0, seq, :, head : head + 1] = grad_beta * beta * (1.0 - beta)
            grad_gram = -beta * grad_lower - jnp.where(row < col, upper[:, CHUNK:], 0.0)
            grad_scores = jnp.where(row >= col, lower[:CHUNK], 0.0)
            by_keys.append(
                dot_nn(
                    jnp.concatenate([narrow(grad_scores), narrow(grad_gram)], axis=0), keys[index]
                )
            )
        by_queries = [
            dot_nn(jnp.where(row <= col, upper[:, :CHUNK], 0.0), query)
            for upper, query in zip(uppers, queries)
        ]
        for index, (seq, head, lanes) in enumerate(chains):
            by_key, by_state, scale = by_keys[index], by_states[index], scales[index]
            grad_query = by_key[:CHUNK] + by_state[:CHUNK]
            grad_key = by_key[CHUNK:] - by_state[CHUNK:] + by_queries[index] + by_laters[index]
            along = jnp.sum(lengths[index] * grad_key, axis=-1, keepdims=True)
            grad_key = scale * (grad_key - lengths[index] * (scale * scale * along))
            for position, grad_act in enumerate((grad_query, grad_key, grad_remains[index])):
                trailing[seq, position, pl.ds(0, CHUNK), lanes] = grad_act * slopes[index][position]
        for seq, head, lanes in chains:
            for position in range(3):
                kept = trailing[seq, position, pl.ds(0, CHUNK), lanes]
                total = None
                for offset in range(4):
                    taps_sum[position, offset, :, lanes] += fold_rows(
                        kept * padded[seq, position, pl.ds(5 + offset, CHUNK), lanes]
                    )
                    term = taps[position, offset : offset + 1, lanes] * trailing[
                        seq, position, pl.ds(3 - offset, CHUNK), lanes
                    ]
                    total = term if total is None else total + term
                grad_projected[position, 0, seq, :, lanes] = narrow(total)

    @pl.when(step == last)
    def _():
        grad_state_out[...] = grad_state[...]
        after_out[...] = trailing[:, :, pl.ds(0, 8), :]
        grad_taps[...] = jnp.sum(taps_sum[...], axis=2)
        grad_gain[...] = jnp.sum(gain_sum[...], axis=0, keepdims=True)


def specs_for(shape, at):
    _, seqs, _, channels = shape

    def rows(width=channels):
        return pl.BlockSpec((1, seqs, CHUNK, width), lambda t, o: (o[0, at(t)], 0, o[1, at(t)], 0))

    planes = pl.BlockSpec(
        (4, 1, seqs, CHUNK, channels), lambda t, o: (0, o[0, at(t)], 0, o[1, at(t)], 0)
    )

    def whole(*shape):
        return pl.BlockSpec(shape, lambda t, o: (0,) * len(shape))

    return rows, planes, whole


def delta_forward(order, projected, logits, taps, gain, state_in, halo_in):
    shape = projected.shape[1:]
    seqs, channels = shape[1], shape[3]
    heads = channels // HEAD_DIM
    steps = shape[0] * shape[2] // CHUNK
    rows, planes, whole = specs_for(shape, lambda t: t)
    return pl.pallas_call(
        forward_kernel,
        out_shape=[
            jax.ShapeDtypeStruct(shape, dtype) for dtype in (BF16, F32, BF16, F32, BF16)
        ]
        + [jax.ShapeDtypeStruct((seqs, heads, HEAD_DIM, HEAD_DIM), F32)],
        grid_spec=pltpu.PrefetchScalarGridSpec(
            num_scalar_prefetch=1,
            grid=(steps,),
            in_specs=[
                planes,
                rows(heads),
                whole(3, 4, channels),
                whole(1, HEAD_DIM),
                whole(seqs, heads, HEAD_DIM, HEAD_DIM),
                whole(seqs, 3, 8, channels),
            ],
            out_specs=[rows() for _ in range(5)] + [whole(seqs, heads, HEAD_DIM, HEAD_DIM)],
            scratch_shapes=[
                pltpu.VMEM((seqs, heads, HEAD_DIM, HEAD_DIM), F32),
                pltpu.VMEM((seqs, 3, CHUNK + 8, channels), F32),
            ],
        ),
        compiler_params=pltpu.CompilerParams(
            dimension_semantics=("arbitrary",), vmem_limit_bytes=56 * 2**20
        ),
        cost_estimate=BRIEF,
        name="delta_forward",
    )(order, projected, logits, taps, gain, state_in, halo_in)


def delta_backward(
    order, projected, logits, taps, gain, halo_in, grad_gated, saved, grad_state_in, after_in
):
    shape = projected.shape[1:]
    seqs, channels = shape[1], shape[3]
    heads = channels // HEAD_DIM
    steps = shape[0] * shape[2] // CHUNK
    rows, planes, whole = specs_for(shape, lambda t: steps - 1 - t)
    part = CHUNK // 8

    def at_before(t, o):
        place = jnp.maximum(steps - 2 - t, 0)
        return (0, o[0, place], 0, o[1, place] * part + part - 1, 0)

    state_block = whole(seqs, heads, HEAD_DIM, HEAD_DIM)
    edge_block = whole(seqs, 3, 8, channels)
    return pl.pallas_call(
        backward_kernel,
        out_shape=[
            jax.ShapeDtypeStruct((4,) + shape, BF16),
            jax.ShapeDtypeStruct(shape[:3] + (heads,), F32),
            jax.ShapeDtypeStruct((3, 4, channels), F32),
            jax.ShapeDtypeStruct((1, HEAD_DIM), F32),
            jax.ShapeDtypeStruct((seqs, heads, HEAD_DIM, HEAD_DIM), F32),
            jax.ShapeDtypeStruct((seqs, 3, 8, channels), F32),
        ],
        grid_spec=pltpu.PrefetchScalarGridSpec(
            num_scalar_prefetch=1,
            grid=(steps,),
            in_specs=[
                planes,
                pl.BlockSpec((3, 1, seqs, 8, channels), at_before),
                rows(heads),
                whole(3, 4, channels),
                whole(1, HEAD_DIM),
                edge_block,
            ]
            + [rows() for _ in range(5)]
            + [state_block, edge_block],
            out_specs=[
                planes,
                rows(heads),
                whole(3, 4, channels),
                whole(1, HEAD_DIM),
                state_block,
                edge_block,
            ],
            scratch_shapes=[
                pltpu.VMEM((seqs, heads, HEAD_DIM, HEAD_DIM), F32),
                pltpu.VMEM((seqs, 3, CHUNK + 8, channels), F32),
                pltpu.VMEM((seqs, 3, CHUNK + 8, channels), F32),
                pltpu.VMEM((3, 4, 8, channels), F32),
                pltpu.VMEM((8, HEAD_DIM), F32),
            ],
        ),
        compiler_params=pltpu.CompilerParams(
            dimension_semantics=("arbitrary",), vmem_limit_bytes=60 * 2**20
        ),
        cost_estimate=BRIEF,
        name="delta_backward",
    )(
        order,
        projected,
        projected,
        logits,
        taps,
        gain,
        halo_in,
        grad_gated,
        *saved,
        grad_state_in,
        after_in,
    )


def weight_kernel(left_count, right_count, planes, deps, order, *refs):
    lefts, rights = refs[: 4 * left_count], refs[4 * left_count : 4 * left_count + right_count]
    outs, turned = refs[4 * left_count + right_count + deps : -1], refs[-1]
    rows, columns = lefts[0].shape

    @pl.when(pl.program_id(0) == 0)
    def _():
        for piece in range(left_count):
            for outer in range(4):
                turned[pl.ds(outer * columns, columns), pl.ds(piece * rows, rows)] = lefts[
                    4 * piece + outer
                ][...].T

    total = None
    size = turned.shape[1] // right_count
    for piece in range(right_count):
        right = rights[piece][0] if planes else rights[piece][...]
        term = lax.dot_general(
            turned[:, pl.ds(piece * size, size)],
            right,
            (((1,), (0,)), ((), ())),
            preferred_element_type=F32,
        )
        total = term if total is None else total + term
    total = narrow(total)
    for plane, out in enumerate(outs):

        @pl.when(pl.program_id(0) == plane)
        def _():
            for outer in range(4):
                out[outer] = total[outer * columns : (outer + 1) * columns]


def weight_products(order, lefts, rights, deps=()):
    rows, width = lefts[0].shape
    all_rows = rows * len(lefts)
    columns = width // 8
    planes, right_rows, size = rights[0].shape

    def pick(outer):
        return lambda n, order: (0, order[outer])

    return pl.pallas_call(
        functools.partial(weight_kernel, len(lefts), len(rights), planes, len(deps)),
        out_shape=[jax.ShapeDtypeStruct((4, columns, size), BF16)] * planes,
        grid_spec=pltpu.PrefetchScalarGridSpec(
            num_scalar_prefetch=1,
            grid=(planes,),
            in_specs=[
                pl.BlockSpec((rows, columns), pick(outer), pipeline_mode=pl.Buffered(1))
                for _ in lefts
                for outer in range(4)
            ]
            + [pl.BlockSpec((1, right_rows, size), lambda n, order: (n, 0, 0))] * len(rights)
            + [pl.BlockSpec(memory_space=pl.ANY)] * len(deps),
            out_specs=[pl.BlockSpec((4, columns, size), lambda n, order: (0, 0, 0))] * planes,
            scratch_shapes=[pltpu.VMEM((4 * columns, all_rows), BF16)],
        ),
        compiler_params=pltpu.CompilerParams(
            dimension_semantics=("arbitrary",), vmem_limit_bytes=60 * 2**20
        ),
        cost_estimate=BRIEF,
        name="weight_products",
    )(order, *[left for left in lefts for _ in range(4)], *rights, *deps)


def feed_kernel(blocks, deps, *refs):
    normed_refs, grad_refs = refs[:blocks], refs[blocks : 2 * blocks]
    w_up_hbm, w_down_hbm = refs[2 * blocks : 2 * blocks + 2]
    refs = refs[2 * blocks + 2 + deps :]
    hidden, gate_grad, out, back = refs[:4]
    w_up, w_down, normed_rows, grad_rows, row_sems, sems = refs[4:]
    step = pl.program_id(0)
    slot = step % 2
    weights = [
        pltpu.make_async_copy(w_up_hbm.at[0], w_up.at[0], sems.at[0]),
        pltpu.make_async_copy(w_up_hbm.at[1], w_up.at[1], sems.at[1]),
        pltpu.make_async_copy(w_down_hbm, w_down, sems.at[2]),
    ]

    def fetch(place, into):
        return [
            pltpu.make_async_copy(normed_refs[place], normed_rows.at[into], row_sems.at[0, into]),
            pltpu.make_async_copy(grad_refs[place], grad_rows.at[into], row_sems.at[1, into]),
        ]

    @pl.when(step == 0)
    def _():
        first = fetch(0, 0)
        first[0].start()
        weights[0].start()
        weights[1].start()
        first[1].start()
        weights[2].start()

    for here in range(1, blocks):

        @pl.when(step == here - 1)
        def _():
            for copy in fetch(here, here % 2):
                copy.start()

    arrived = fetch(0, slot)
    arrived[0].wait()

    @pl.when(step == 0)
    def _():
        weights[0].wait()

    normed = normed_rows[slot]
    gate = dot_nn(normed, w_up[0])

    @pl.when(step == 0)
    def _():
        weights[1].wait()

    up = dot_nn(normed, w_up[1])
    arrived[1].wait()

    @pl.when(step == 0)
    def _():
        weights[2].wait()

    grad_hidden = dot_nt(grad_rows[slot], w_down[...])
    sig = sigmoid(gate)
    act = gate * sig
    inner = narrow(act * up)
    gate_back = narrow(grad_hidden * up * slope(gate, sig))
    up_back = narrow(grad_hidden * act)
    hidden[...] = inner
    gate_grad[0] = gate_back
    gate_grad[1] = up_back
    out[...] = narrow(dot_nn(inner, w_down[...]))
    back[...] = narrow(dot_nt(gate_back, w_up[0]) + dot_nt(up_back, w_up[1]))


def feed_forward(normed, grads, w_up, w_down, deps=()):
    blocks = len(normed)
    rows, width = normed[0].shape
    size = w_down.shape[0]
    anywhere = pl.BlockSpec(memory_space=pl.ANY)
    wide = jax.ShapeDtypeStruct((rows * blocks, width), BF16)
    return pl.pallas_call(
        functools.partial(feed_kernel, blocks, len(deps)),
        out_shape=[
            jax.ShapeDtypeStruct((rows * blocks, size), BF16),
            jax.ShapeDtypeStruct((2, rows * blocks, size), BF16),
            wide,
            wide,
        ],
        grid=(blocks,),
        in_specs=[anywhere] * (2 * blocks + 2 + len(deps)),
        out_specs=[
            pl.BlockSpec((rows, size), lambda i: (i, 0)),
            pl.BlockSpec((2, rows, size), lambda i: (0, i, 0)),
            pl.BlockSpec((rows, width), lambda i: (i, 0)),
            pl.BlockSpec((rows, width), lambda i: (i, 0)),
        ],
        scratch_shapes=[
            pltpu.VMEM((2, width, size), BF16),
            pltpu.VMEM((size, width), BF16),
            pltpu.VMEM((2, rows, width), BF16),
            pltpu.VMEM((2, rows, width), BF16),
            pltpu.SemaphoreType.DMA((2, 2)),
            pltpu.SemaphoreType.DMA((3,)),
        ],
        compiler_params=pltpu.CompilerParams(
            dimension_semantics=("arbitrary",), vmem_limit_bytes=60 * 2**20
        ),
        cost_estimate=BRIEF,
        name="feed_forward",
    )(*normed, *grads, w_up, w_down, *deps)


def rows_kernel(blocks, planes, transposed, deps, *refs):
    row_refs, weight_hbm = refs[:blocks], refs[blocks]
    out, weight, now, row_sems, sems = refs[blocks + 1 + deps :]
    step = pl.program_id(0)
    slot = step % 2
    loads = [
        pltpu.make_async_copy(weight_hbm.at[plane], weight.at[plane], sems.at[plane])
        for plane in range(planes)
    ]

    def fetch(place, into):
        return pltpu.make_async_copy(row_refs[place], now.at[into], row_sems.at[into])

    @pl.when(step == 0)
    def _():
        fetch(0, 0).start()
        for load in loads:
            load.start()

    for here in range(1, blocks):

        @pl.when(step == here - 1)
        def _():
            fetch(here, here % 2).start()

    fetch(0, slot).wait()
    value = now[slot]
    for plane in range(planes):

        @pl.when(step == 0)
        def _():
            loads[plane].wait()

        out[plane] = (dot_nt if transposed else dot_nn)(value, weight[plane]).astype(out.dtype)


def rows_product(blocks, weight, transposed, dtype, deps=()):
    rows, width = blocks[0].shape
    planes = weight.shape[0]
    size = weight.shape[1] if transposed else weight.shape[2]
    anywhere = pl.BlockSpec(memory_space=pl.ANY)
    count = len(blocks)
    return pl.pallas_call(
        functools.partial(rows_kernel, count, planes, transposed, len(deps)),
        out_shape=jax.ShapeDtypeStruct((planes, rows * count, size), dtype),
        grid=(count,),
        in_specs=[anywhere] * (count + 1 + len(deps)),
        out_specs=pl.BlockSpec((planes, rows, size), lambda i: (0, i, 0)),
        scratch_shapes=[
            pltpu.VMEM(weight.shape, BF16),
            pltpu.VMEM((2, rows, width), BF16),
            pltpu.SemaphoreType.DMA((2,)),
            pltpu.SemaphoreType.DMA((planes,)),
        ],
        compiler_params=pltpu.CompilerParams(
            dimension_semantics=("arbitrary",), vmem_limit_bytes=60 * 2**20
        ),
        cost_estimate=BRIEF,
        name="rows_product",
    )(*blocks, weight, *deps)


def input_kernel(planes, deps, *refs):
    grad, logit, weight_hbm, beta_weight = refs[:4]
    away, near, weight, sems = refs[4 + deps :]
    step = pl.program_id(0)
    loads = [
        pltpu.make_async_copy(weight_hbm.at[plane], weight.at[plane], sems.at[plane])
        for plane in range(planes)
    ]

    @pl.when(step == 0)
    def _():
        for load in loads:
            load.start()

    total = dot_nt(logit[...], beta_weight[...])
    for plane in range(planes):

        @pl.when(step == 0)
        def _():
            loads[plane].wait()

        total = total + dot_nt(grad[plane], weight[plane])
    total = narrow(total)
    half = pl.num_programs(0) // 2

    @pl.when(step < half)
    def _():
        away[...] = total

    @pl.when(step >= half)
    def _():
        near[...] = total


def input_product(grad, logit, weight, beta_weight, block, deps=()):
    planes, rows, size = grad.shape
    width = weight.shape[1]
    count = rows // block
    half = count // 2
    place = lambda i: (i + half) % count
    anywhere = pl.BlockSpec(memory_space=pl.ANY)
    return pl.pallas_call(
        functools.partial(input_kernel, planes, len(deps)),
        out_shape=[jax.ShapeDtypeStruct((rows // 2, width), BF16)] * 2,
        grid=(count,),
        in_specs=[
            pl.BlockSpec((planes, block, size), lambda i: (0, place(i), 0)),
            pl.BlockSpec((block, logit.shape[1]), lambda i: (place(i), 0)),
            anywhere,
            pl.BlockSpec(beta_weight.shape, lambda i: (0, 0)),
        ]
        + [anywhere] * len(deps),
        out_specs=[
            pl.BlockSpec((block, width), lambda i: (jnp.minimum(i, half - 1), 0)),
            pl.BlockSpec((block, width), lambda i: (jnp.maximum(i - half, 0), 0)),
        ],
        scratch_shapes=[pltpu.VMEM(weight.shape, BF16), pltpu.SemaphoreType.DMA((planes,))],
        compiler_params=pltpu.CompilerParams(
            dimension_semantics=("arbitrary",), vmem_limit_bytes=60 * 2**20
        ),
        cost_estimate=BRIEF,
        name="input_product",
    )(grad, logit, weight, beta_weight, *deps)


def rms_scale(signal, gain):
    return signal * lax.rsqrt(jnp.mean(signal * signal, axis=-1, keepdims=True) + EPS) * gain


def rms_back(signal, gain, grad):
    rate = lax.rsqrt(jnp.mean(signal * signal, axis=-1, keepdims=True) + EPS)
    unit = signal * rate
    scaled = grad * gain
    grad_signal = rate * (scaled - unit * jnp.mean(scaled * unit, axis=-1, keepdims=True))
    return grad_signal, jnp.sum(grad * unit, axis=0)


def tie(*values):
    return lax.optimization_barrier(values)


def hold(value, *others):
    return tie(value, *others)[0]


def swap(value, axis, distance):
    size = lax.axis_size(axis)
    return lax.ppermute(value, axis, [(place, place ^ distance) for place in range(size)])


def sum_over(value, axis):
    distance = 1
    while distance < lax.axis_size(axis):
        value = value + swap(value, axis, distance)
        distance *= 2
    return value


def own_scale(group_ids, group_weight, seqs_here, own_seq):
    group_range = jnp.arange(GROUPS, dtype=jnp.int32)
    member = (group_ids[:, None] == group_range[None, :]).astype(jnp.int32)
    counts = sum_over(jnp.sum(member, axis=0) * LEN, "dp").astype(F32)
    member_float = member.astype(F32)
    seq_weight = jnp.sum(member_float * group_weight.astype(F32)[None, :], axis=1)
    seq_count = jnp.sum(member_float * counts[None, :], axis=1)
    total_tokens = LEN * seqs_here * lax.axis_size("dp")
    seq_scale = seq_weight * total_tokens / (GROUPS * seq_count)
    return jnp.sum(jnp.where(jnp.arange(seqs_here) == own_seq, seq_scale, 0.0))


def sum_small(grad_beta, grad_taps, gain_one, gain_two, gain_heads):
    beta_size, taps_size, width = grad_beta.size, grad_taps.size, gain_one.size
    small = sum_over(
        jnp.concatenate(
            [grad_beta.reshape(-1), grad_taps.reshape(-1), gain_one, gain_two, gain_heads]
        ),
        "dp",
    )
    gains = sum_over(small[beta_size + taps_size :], "head")
    return (
        small[:beta_size].reshape(grad_beta.shape),
        small[beta_size : beta_size + taps_size].reshape(grad_taps.shape),
        gains[:width],
        gains[width : 2 * width],
        gains[2 * width :],
    )


def plain_body(
    tokens,
    norm_gain,
    w_proj,
    w_beta,
    conv_weight,
    head_gain,
    w_out,
    ffn_gain,
    w_ffn,
    w_down,
    group_ids,
    group_weight,
    cotangent,
):
    rows_here = tokens.shape[0]
    head_pos = lax.axis_index("head")
    seqs = rows_here * lax.axis_size("head") // LEN
    channels = w_proj.shape[2]
    heads = channels // HEAD_DIM
    gain_one, gain_two = norm_gain.astype(F32), ffn_gain.astype(F32)
    gain_heads, taps = head_gain.astype(F32)[None], conv_weight.astype(F32)

    def gather(rows):
        return lax.all_gather(narrow(rows), "head", axis=0, tiled=True)

    def scatter(partial):
        return lax.psum_scatter(narrow(partial), "head", scatter_dimension=0, tiled=True).astype(F32)

    def scatter_weight(product, dim):
        return lax.psum_scatter(narrow(product), "dp", scatter_dimension=dim, tiled=True).astype(F32)

    def product(form, left, right):
        return jnp.einsum(form, left, right, preferred_element_type=F32)

    x_here = tokens.astype(F32)
    scale = own_scale(group_ids, group_weight, seqs, (head_pos * rows_here) // LEN)
    upstream = cotangent.astype(F32) * scale
    normed = gather(rms_scale(x_here, gain_one))
    grad_ffn = gather(upstream)
    steps = LEN // CHUNK
    order = jnp.stack([jnp.zeros(steps, jnp.int32), jnp.arange(steps, dtype=jnp.int32)])

    def by_seq(rows):
        return rows.reshape(rows.shape[:-2] + (1, seqs, LEN, rows.shape[-1]))

    def flat(rows):
        return rows.reshape(rows.shape[:-4] + (seqs * LEN, rows.shape[-1]))

    projected = by_seq(product("td,fdk->ftk", normed, w_proj))
    logits = by_seq(product("td,dh->th", normed, w_beta))
    state = jnp.zeros((seqs, heads, HEAD_DIM, HEAD_DIM), F32)
    halo = jnp.zeros((seqs, 3, 8, channels), F32)
    gated, *saved, _ = delta_forward(order, projected, logits, taps, gain_heads, state, halo)
    gated = flat(gated)
    middle = x_here + scatter(product("tk,kd->td", gated, w_out))
    normed_two = gather(rms_scale(middle, gain_two))
    gate_up = product("td,fdk->ftk", normed_two, w_ffn)
    grad_hidden = product("td,fd->tf", grad_ffn, w_down)
    sig = sigmoid(gate_up[0])
    act = gate_up[0] * sig
    hidden = narrow(act * gate_up[1])
    gate_grad = jnp.stack(
        [narrow(grad_hidden * gate_up[1] * slope(gate_up[0], sig)), narrow(grad_hidden * act)]
    )
    mixed_out = narrow(middle + scatter(product("tk,kd->td", hidden, w_down)))
    through, gain_two_sum = rms_back(
        middle, gain_two, scatter(product("ftk,fdk->td", gate_grad, w_ffn))
    )
    grad_middle = upstream + through
    grad_mixer = gather(grad_middle)
    back, logit_back, taps_back, gain_back, _, _ = delta_backward(
        order,
        projected,
        logits,
        taps,
        gain_heads,
        halo,
        by_seq(product("td,kd->tk", grad_mixer, w_out)),
        saved,
        state,
        halo,
    )
    back, logit_back = flat(back), narrow(flat(logit_back))
    grad_normed = scatter(
        product("ftk,fdk->td", back, w_proj) + product("th,dh->td", logit_back, w_beta)
    )
    through, gain_one_sum = rms_back(x_here, gain_one, grad_normed)
    beta, conv, gain_one_sum, gain_two_sum, gain_back = sum_small(
        product("td,th->dh", normed, logit_back), taps_back, gain_one_sum, gain_two_sum, gain_back[0]
    )
    return (
        mixed_out,
        grad_middle + through,
        gain_one_sum,
        scatter_weight(product("td,ftk->fdk", normed, back), 1),
        beta,
        conv,
        gain_back,
        scatter_weight(product("tk,td->kd", gated, grad_mixer), 1),
        gain_two_sum,
        scatter_weight(product("td,ftk->fdk", normed_two, gate_grad), 1),
        scatter_weight(product("tf,td->fd", hidden, grad_ffn), 1),
    )


def pair_sum(away, near):
    return near.astype(F32) + swap(away, "head", 1).astype(F32)


def own_half(total):
    return total[: total.shape[0] // 2]


def far_half(total):
    return swap(narrow(total[total.shape[0] // 2 :]), "head", 2)


def paired_body(
    tokens,
    norm_gain,
    w_proj,
    w_beta,
    conv_weight,
    head_gain,
    w_out,
    ffn_gain,
    w_ffn,
    w_down,
    group_ids,
    group_weight,
    cotangent,
):
    rows_here, width = tokens.shape
    head_pos = lax.axis_index("head")
    core = head_pos % 2
    place = lax.axis_index("dp")
    outer, inner = place // 2, place % 2
    seqs = 2
    channels = w_proj.shape[2]
    heads = channels // HEAD_DIM
    half = rows_here // 2
    gain_one, gain_two = norm_gain.astype(F32), ffn_gain.astype(F32)
    gain_heads, taps = head_gain.astype(F32)[None], conv_weight.astype(F32)

    def deal(rows):
        first, second = rows[:half], rows[half:]
        other = swap(jnp.where(core == 0, second, first), "head", 1)
        return jnp.where(core == 0, first, other), jnp.where(core == 0, other, second)

    def undeal(early, late):
        other = swap(jnp.where(core == 0, late, early), "head", 1)
        return jnp.concatenate(
            [jnp.where(core == 0, early, other), jnp.where(core == 0, other, late)], axis=0
        )

    def product(left, right):
        return jnp.dot(left, right, preferred_element_type=F32)

    split = half // CHUNK
    step_range = jnp.arange(2 * split, dtype=jnp.int32)
    order = jnp.stack([(step_range // split) ^ core, step_range % split])

    def by_seq(rows):
        return rows.reshape(rows.shape[:-2] + (2, seqs, half, rows.shape[-1]))

    def flat(rows):
        return rows.reshape(rows.shape[:-4] + (2 * seqs * half, rows.shape[-1]))

    near_order = 2 * (outer ^ jnp.array([0, 2, 1, 3], dtype=jnp.int32)) + inner
    away_order = near_order ^ 1

    def far_of(rows):
        return swap(rows, "head", 2)

    def blocks(rows, far):
        return [rows, far, swap(rows, "head", 1), swap(far, "head", 1)]

    def logits_of(normed):
        return jnp.concatenate([product(block, w_beta) for block in normed], axis=0)

    def mixer_out(gated):
        count = gated.shape[0] // 2
        return pair_sum(narrow(product(gated[count:], w_out)), product(gated[:count], w_out))

    def send(products):
        return [swap(value, "dp", 1) for value in products]

    def halve(kept, away):
        return swap(narrow(kept[2:].astype(F32) + away[2:].astype(F32)), "dp", 2)

    def halve_again(kept, away, first):
        return swap(
            narrow(kept[1].astype(F32) + away[1].astype(F32) + first[1].astype(F32)), "dp", 4
        )

    def finish(kept, away, first, second):
        return (
            kept[0].astype(F32) + away[0].astype(F32) + first[0].astype(F32) + second.astype(F32)
        )

    x_a, x_b = [part.astype(F32) for part in deal(tokens)]
    rows_a, rows_b = narrow(rms_scale(x_a, gain_one)), narrow(rms_scale(x_b, gain_one))
    far_a = far_of(rows_a)
    normed_a = blocks(rows_a, far_a)
    scale = own_scale(group_ids, group_weight, seqs, head_pos // 2)
    up_a, up_b = [part.astype(F32) * scale for part in deal(cotangent)]
    up_rows_a, up_rows_b = narrow(up_a), narrow(up_b)
    far_b = far_of(rows_b)
    up_far_a = far_of(hold(up_rows_a, far_a))

    state = jnp.zeros((seqs, heads, HEAD_DIM, HEAD_DIM), F32)
    halo_a = jnp.zeros((seqs, 3, 8, channels), F32)
    projected_a = by_seq(rows_product(normed_a, w_proj, False, F32))
    logits_a = by_seq(logits_of(normed_a))
    gated_a, *saved_a, state_a = delta_forward(
        order, projected_a, logits_a, taps, gain_heads, state, halo_a
    )
    gated_a = flat(gated_a)
    halo_b = lax.dynamic_slice(
        projected_a, (0, 1 - core, 0, half - 8, 0), (3, 1, seqs, 8, channels)
    )[:, 0].transpose(1, 0, 2, 3)
    gated_a, far_b, up_far_a = lax.optimization_barrier((gated_a, far_b, up_far_a))
    mixer_a = mixer_out(gated_a)
    mixer_far_a = far_half(mixer_a)
    up_far_b = far_of(hold(up_rows_b, mixer_a))

    normed_b = blocks(rows_b, far_b)
    grad_ffn_a = blocks(up_rows_a, up_far_a)
    projected_b = by_seq(rows_product(hold(normed_b, mixer_a), w_proj, False, F32))
    logits_b = by_seq(logits_of(normed_b))
    gated_b, *saved_b, _ = delta_forward(
        order, projected_b, logits_b, taps, gain_heads, state_a, halo_b
    )
    gated_b = flat(gated_b)
    gated_b, mixer_far_a, up_far_b = lax.optimization_barrier((gated_b, mixer_far_a, up_far_b))
    middle_a = x_a + own_half(mixer_a) + mixer_far_a.astype(F32)
    rows_a = narrow(rms_scale(middle_a, gain_two))
    two_far_a = far_of(rows_a)
    mixer_b = mixer_out(hold(gated_b, rows_a))
    mixer_far_b = far_half(mixer_b)
    two_a = blocks(rows_a, hold(two_far_a, mixer_b))
    grad_ffn_b = blocks(up_rows_b, up_far_b)

    def feed(normed, grads):
        return feed_forward(normed, grads, w_ffn, w_down)

    away_a = feed(two_a[2:], grad_ffn_a[2:])
    away_a, mixer_far_b = lax.optimization_barrier((away_a, mixer_far_b))
    middle_b = x_b + own_half(mixer_b) + mixer_far_b.astype(F32)
    rows_b = narrow(rms_scale(middle_b, gain_two))
    two_far_b = far_of(rows_b)
    near_a = feed(hold(two_a[:2], rows_b), grad_ffn_a[:2])
    near_a, two_far_b = lax.optimization_barrier((near_a, two_far_b))
    back_a = pair_sum(away_a[3], near_a[3])
    back_far_a = far_half(back_a)
    out_a = pair_sum(away_a[2], hold(near_a[2], back_a))
    out_far_a = far_half(out_a)
    two_b = blocks(rows_b, two_far_b)
    away_b = feed(hold(two_b[2:], back_a, out_a), grad_ffn_b[2:])
    away_b, back_far_a = lax.optimization_barrier((away_b, back_far_a))
    through, gain_two_a = rms_back(middle_a, gain_two, own_half(back_a) + back_far_a.astype(F32))
    grad_middle_a = up_a + through
    mix_rows_a = narrow(grad_middle_a)
    mix_far_a = far_of(mix_rows_a)
    near_b = feed(hold(two_b[:2], mix_rows_a), grad_ffn_b[:2])
    near_b, mix_far_a, out_far_a = lax.optimization_barrier((near_b, mix_far_a, out_far_a))
    back_b = pair_sum(away_b[3], near_b[3])
    back_far_b = far_half(back_b)

    down_left = grad_ffn_a + grad_ffn_b
    down_right = [part[0][None] for part in (near_a, away_a, near_b, away_b)]
    up_left = two_a + two_b
    up_right = [part[1] for part in (near_a, away_a, near_b, away_b)]
    down_sent = weight_products(hold(away_order, back_b), down_left, down_right)
    (down_away,) = send(down_sent)
    up_sent = weight_products(hold(away_order, *down_sent), up_left, up_right)
    up_sent, back_far_b = lax.optimization_barrier((up_sent, back_far_b))
    up_away_0, up_away_1 = send(up_sent)
    through, gain_two_b = rms_back(middle_b, gain_two, own_half(back_b) + back_far_b.astype(F32))
    grad_middle_b = up_b + through
    mix_rows_b = narrow(grad_middle_b)
    mix_far_b = far_of(mix_rows_b)
    out_b = pair_sum(away_b[2], hold(near_b[2], mix_rows_b))
    out_far_b = far_half(out_b)
    (down_kept,) = weight_products(hold(near_order, mix_rows_b, out_b), down_left, down_right)
    w_out_plane = w_out[None]
    grad_mixer_a = blocks(mix_rows_a, mix_far_a)
    grad_gated_a = rows_product(hold(grad_mixer_a, down_kept), w_out_plane, True, F32)[0]
    grad_gated_a, mix_far_b = lax.optimization_barrier((grad_gated_a, mix_far_b))
    grad_mixer_b = blocks(mix_rows_b, mix_far_b)
    grad_gated_b = rows_product(hold(grad_mixer_b, grad_gated_a), w_out_plane, True, F32)[0]
    grad_gated_b, down_away = lax.optimization_barrier((grad_gated_b, down_away))
    down_first = halve(down_kept, down_away)

    zero_state = jnp.zeros((seqs, heads, HEAD_DIM, HEAD_DIM), F32)
    zero_after = jnp.zeros((seqs, 3, 8, channels), F32)
    late = delta_backward(
        order,
        projected_b,
        logits_b,
        taps,
        gain_heads,
        halo_b,
        by_seq(grad_gated_b),
        saved_b,
        zero_state,
        zero_after,
    )
    late, down_first, out_far_b = tie(late, down_first, out_far_b)
    proj_b, logit_b, taps_b, gain_heads_b, grad_state, after = late
    down_second = halve_again(down_kept, down_away, down_first)
    up_kept_0, up_kept_1 = weight_products(hold(near_order, grad_state), up_left, up_right)
    up_kept_0, up_kept_1, up_away_0 = lax.optimization_barrier((up_kept_0, up_kept_1, up_away_0))
    up_first_0 = halve(up_kept_0, up_away_0)
    out_left, out_right = grad_mixer_a + grad_mixer_b, [gated_a[None], gated_b[None]]
    (out_sent,) = weight_products(hold(away_order, up_kept_0), out_left, out_right)
    (out_away,) = send([out_sent])
    early = delta_backward(
        order,
        projected_a,
        logits_a,
        taps,
        gain_heads,
        halo_a,
        by_seq(grad_gated_a),
        saved_a,
        hold(grad_state, out_sent),
        after,
    )
    proj_a, logit_a, taps_a, gain_heads_a, _, _ = early
    proj_a, proj_b = flat(proj_a), flat(proj_b)
    logit_a, logit_b = narrow(flat(logit_a)), narrow(flat(logit_b))
    proj_left, proj_right = normed_a + normed_b, [proj_a, proj_b]
    proj_sent = weight_products(away_order, proj_left, proj_right)
    proj_sent, up_away_1, proj_a, up_first_0, down_second = tie(
        proj_sent, up_away_1, proj_a, up_first_0, down_second
    )
    proj_away = send(proj_sent)
    up_second_0 = halve_again(up_kept_0, up_away_0, up_first_0)
    up_first_1 = halve(up_kept_1, up_away_1)
    inputs_a = input_product(proj_a, logit_a, w_proj, w_beta, half)
    inputs_a, out_away, proj_b = tie(inputs_a, out_away, proj_b)
    inputs_b = input_product(proj_b, logit_b, w_proj, w_beta, half)
    inputs_a, inputs_b, proj_away[0], proj_away[1], up_first_1 = tie(
        inputs_a, inputs_b, proj_away[0], proj_away[1], up_first_1
    )
    in_a = pair_sum(*inputs_a)
    in_b = pair_sum(*inputs_b)
    up_quarter_1 = narrow(
        up_kept_1[1].astype(F32) + up_away_1[1].astype(F32) + up_first_1[1].astype(F32)
    )
    in_a, in_b, near_order, up_quarter_1 = tie(in_a, in_b, near_order, up_quarter_1)
    up_second_1 = swap(up_quarter_1, "dp", 4)
    in_far_a = far_half(in_a)
    in_far_b = far_half(in_b)
    proj_kept = weight_products(near_order, proj_left, proj_right)
    proj_kept, proj_away[2], near_order = tie(proj_kept, proj_away[2], near_order)
    proj_first = [halve(kept, away) for kept, away in zip(proj_kept[:2], proj_away[:2])]
    (out_kept,) = weight_products(near_order, out_left, out_right)
    out_kept, proj_away[3], out_a, out_b = tie(out_kept, proj_away[3], out_a, out_b)
    proj_first += [halve(kept, away) for kept, away in zip(proj_kept[2:], proj_away[2:])]
    out_first = halve(out_kept, out_away)
    proj_second = [
        halve_again(kept, away, first)
        for kept, away, first in zip(proj_kept, proj_away, proj_first)
    ]
    out_second = halve_again(out_kept, out_away, out_first)

    mixed_out = undeal(
        narrow(middle_a + own_half(out_a) + out_far_a.astype(F32)),
        narrow(middle_b + own_half(out_b) + out_far_b.astype(F32)),
    )
    through_b, gain_one_b = rms_back(x_b, gain_one, own_half(in_b) + in_far_b.astype(F32))
    through_a, gain_one_a = rms_back(x_a, gain_one, own_half(in_a) + in_far_a.astype(F32))
    grad_tokens = undeal(grad_middle_a + through_a, grad_middle_b + through_b)
    grad_beta = 0.0
    for normed, logit in ((normed_a, logit_a), (normed_b, logit_b)):
        for index, block in enumerate(normed):
            grad_beta = grad_beta + jnp.einsum(
                "td,th->dh",
                block,
                logit[index * half : (index + 1) * half],
                preferred_element_type=F32,
            )
    beta, conv, gain_one_sum, gain_two_sum, gain_heads_sum = sum_small(
        grad_beta,
        taps_a + taps_b,
        gain_one_a + gain_one_b,
        gain_two_a + gain_two_b,
        (gain_heads_a + gain_heads_b)[0],
    )
    return (
        mixed_out,
        grad_tokens,
        gain_one_sum,
        jnp.stack(
            [finish(*parts) for parts in zip(proj_kept, proj_away, proj_first, proj_second)]
        ),
        beta,
        conv,
        gain_heads_sum,
        finish(out_kept, out_away, out_first, out_second).T,
        gain_two_sum,
        jnp.stack(
            [
                finish(up_kept_0, up_away_0, up_first_0, up_second_0),
                finish(up_kept_1, up_away_1, up_first_1, up_second_1),
            ]
        ),
        finish(down_kept, down_away, down_first, down_second).T,
    )


def body(*args):
    rows_here, channels = args[0].shape[0], args[2].shape[2]
    paired = (
        lax.axis_size("head") == 4
        and lax.axis_size("dp") == 8
        and rows_here * 2 == LEN
        and channels % HEAD_DIM == 0
    )
    return (paired_body if paired else plain_body)(*args)


def solution(mesh):
    placed = (
        P(("dp", "head"), None),
        P(),
        P(None, None, "head"),
        P(None, "head"),
        P(None, None, "head"),
        P(),
        P("head", None),
        P(),
        P(None, None, "head"),
        P("head", None),
        P("dp"),
        P(),
        P(("dp", "head"), None),
    )
    return jax.shard_map(
        body,
        mesh=mesh,
        in_specs=placed,
        out_specs=(
            P(("dp", "head"), None),
            P(("dp", "head"), None),
            P(),
            P(None, "dp", "head"),
            P(None, "head"),
            P(None, None, "head"),
            P(),
            P("head", "dp"),
            P(),
            P(None, "dp", "head"),
            P("head", "dp"),
        ),
        check_vma=False,
    )
```
